32 devices in a mesh: row: 4 (over y, x), col: 8 (over z, core).
Axes of the slice: x: 2, y: 2, z: 4, core: 2. Of those that a mesh axis runs over, the one named last changes fastest.
Arguments:
- iterate: bfloat16 [4096, 6144], P(('row', 'col')), may hold values from -0.25 to 0.25
Outputs:
- update: bfloat16 [4096, 6144], P('row', 'col')
The draws below stay inside these ranges and needn't reach their ends.
All inputs are finite; a program needn't handle non-finite values.
Results may differ from the reference program's by a relative error of at most 0.0084.
Values may be sent and summed in bfloat16 or wider, within the bound.
No kernel may reach another device: no remote copies, remote signals or barrier semaphores. Data moves between devices by JAX's collectives and lax.ppermute only.
A program may use at most 64 MiB of HBM per device.

```python
import math
import jax
import jax.numpy as jnp
from jax import lax

M = 4096
D = 6144


def draw_iterate(key, part):
    folded = jax.random.fold_in(key, 17)
    key_base, key_rows, key_cols = jax.random.split(folded, 3)
    spread_log = math.log(2.0)
    base_field = jnp.clip(jax.random.normal(key_base, (M, D), jnp.float32), -6.0, 6.0)
    row_scale = jnp.exp(jax.random.uniform(key_rows, (M, 1), jnp.float32, 0.0, spread_log))
    col_scale = jnp.exp(jax.random.uniform(key_cols, (1, D), jnp.float32, 0.0, spread_log))
    mean_square = (math.exp(2.0 * spread_log) - 1.0) / (2.0 * spread_log)
    factor = 0.6 / (math.sqrt(D) * mean_square)
    return (factor * base_field * row_scale * col_scale).astype(jnp.bfloat16)


def setup_inputs(seed: int = 0) -> dict:
    arg_keys = jax.random.split(jax.random.key(seed), 2)
    return {
        "iterate": draw_iterate(jax.random.fold_in(arg_keys[1], 71), 0),
    }


linear_weight = 3.4445
cubic_weight = -4.775
quintic_weight = 2.0315
output_gain = 0.2

def reference(iterate):
    gram_matrix = lax.dot_general(iterate, iterate, (((1,), (1,)), ((), ())), preferred_element_type=jnp.float32).astype(jnp.bfloat16)
    image_matrix = jnp.dot(gram_matrix, iterate, preferred_element_type=jnp.float32).astype(jnp.bfloat16)
    second_term = jnp.dot(gram_matrix, image_matrix, preferred_element_type=jnp.float32)
    combined = linear_weight * iterate.astype(jnp.float32) + cubic_weight * image_matrix.astype(jnp.float32) + quintic_weight * second_term
    update = (output_gain * math.sqrt(max(M, D)) * combined).astype(jnp.bfloat16)
    return update
```

```python
import math

import jax
import jax.numpy as jnp
from jax import lax
from jax.sharding import PartitionSpec as P

linear_weight = 3.4445
cubic_weight = -4.775
quintic_weight = 2.0315
output_gain = 0.2


def gather_rows(block_rows):
    return lax.all_gather(block_rows, "row", axis=0, tiled=True)


def strided_order(panel_rows, row_devices, col_devices):
    total_rows, column_count = panel_rows.shape
    per_device = total_rows // (row_devices * col_devices)
    grouped = panel_rows.reshape(row_devices, col_devices, per_device, column_count)
    return jnp.transpose(grouped, (1, 0, 2, 3)).reshape(total_rows, column_count)


def row_product(left_rows, right_rows):
    return lax.dot_general(
        left_rows, right_rows, (((1,), (1,)), ((), ())), preferred_element_type=jnp.float32
    )


def combine(scaled_tile, image_tile, second_term, gain):
    combined = (
        linear_weight * scaled_tile.astype(jnp.float32)
        + cubic_weight * image_tile.astype(jnp.float32)
        + quintic_weight * second_term
    )
    return (gain * combined).astype(jnp.bfloat16)


def gathered_plan(iterate, gain):
    scaled_tile = lax.all_to_all(iterate, "col", split_axis=1, concat_axis=0, tiled=True)
    row_devices = lax.axis_size("row")
    col_devices = lax.axis_size("col")
    strided_rows = gather_rows(iterate)
    panel_rows = lax.all_gather(scaled_tile, "col", axis=1, tiled=True)
    gram_tile = row_product(panel_rows, strided_rows).astype(jnp.bfloat16)
    gram_wide = lax.all_gather(gram_tile, "col", axis=1, tiled=True)
    scaled_columns = strided_order(gather_rows(scaled_tile), row_devices, col_devices)
    image_tile = jnp.dot(gram_wide, scaled_columns, preferred_element_type=jnp.float32).astype(
        jnp.bfloat16
    )
    image_columns = strided_order(gather_rows(image_tile), row_devices, col_devices)
    second_term = jnp.dot(gram_wide, image_columns, preferred_element_type=jnp.float32)
    return combine(scaled_tile, image_tile, second_term, gain)


def neighbour_plan(iterate, gain):
    line = lax.axis_size("col") // 2
    count, width = iterate.shape
    slab = width // (2 * line)
    row_devices = lax.axis_size("row")
    place = lax.axis_index("col")
    level, core = place // 2, place % 2

    def along(values, pairs):
        pairs = [(2 * a + k, 2 * b + k) for a, b in pairs for k in range(2)]
        return lax.ppermute(values, "col", pairs)

    def swap(values):
        pairs = [(2 * a + k, 2 * a + 1 - k) for a in range(line) for k in range(2)]
        return lax.ppermute(values, "col", pairs)

    def across(values, bit):
        return lax.ppermute(values, "row", [(i, i ^ bit) for i in range(row_devices)])

    def square(block):
        one, two = across(block, 1), across(block, 2)
        cut = block.shape[0] // 2
        three = [across(one[:cut], 2), across(two[cut:], 1)]
        return block, one, two, jnp.concatenate(three)

    slabs = []
    for step in range(2):
        offset = jnp.where(step == 0, core, 1 - core) * slab
        parts = []
        for hop in range(line):
            start = ((level - hop) % line) * (2 * slab) + offset
            piece = lax.dynamic_slice(iterate, (0, start), (count, slab))
            if hop:
                piece = along(piece, [(a, (a - hop) % line) for a in range(line)])
            parts.append(piece)
        tower = jnp.zeros((line, count, slab), iterate.dtype)
        for hop, piece in enumerate(parts):
            tower = lax.dynamic_update_slice(tower, piece[None], ((level + hop) % line, 0, 0))
        own = square(tower.reshape(line * count, slab))
        slabs.append((own, [swap(block) for block in own]))

    def interleave(mine, other):
        shape = (line, 1, count, slab)
        mine, other = mine.reshape(shape), other.reshape(shape)
        first = jnp.where(core == 0, mine, other)
        last = jnp.where(core == 0, other, mine)
        return jnp.concatenate([first, last], axis=1).reshape(2 * line * count, slab)

    near = jnp.concatenate([interleave(a, b) for a, b in zip(slabs[0][0], slabs[1][1])])
    far = jnp.concatenate([interleave(a, b) for a, b in zip(slabs[1][0], slabs[0][1])])
    total = near.shape[0]

    half = count // 2
    near_rows = slabs[0][0][0].reshape(line, 2, half, slab)
    far_rows = slabs[1][0][0].reshape(line, 2, half, slab)
    gram_parts = []
    for part in range(2):
        left = near_rows[:, part].reshape(line * half, slab)
        right = far_rows[:, part].reshape(line * half, slab)
        product = row_product(left, near) + row_product(right, far)
        gram_parts.append(product.astype(jnp.bfloat16).reshape(line, half, total))

    def reduced(partial):
        up = down = None
        for step in range(1, line):
            def outgoing(index, arrived):
                index = jnp.clip(index, 0, line - 1)
                value = lax.dynamic_index_in_dim(partial, index, 0, keepdims=False)
                return value if arrived is None else value + arrived
            up_value = outgoing(line - step + level, up)
            down_value = outgoing(level + step - line, down)
            up = along(up_value, [(a, a + 1) for a in range(step)])
            down = along(down_value, [(line - 1 - a, line - 2 - a) for a in range(step)])
        own = lax.dynamic_index_in_dim(partial, level, 0, keepdims=False)
        total = own.astype(jnp.float32) + up.astype(jnp.float32) + down.astype(jnp.float32)
        return total.astype(jnp.bfloat16)

    def spread(own):
        ups, downs = [own], [own]
        for step in range(1, line):
            ups.append(along(ups[-1], [(a, a + 1) for a in range(step - 1, line - 1)]))
            downs.append(along(downs[-1], [(a, a - 1) for a in range(1, line - step + 1)]))
        found = [(level, own)]
        order = []
        for a in range(line):
            below, above = a, line - 1 - a
            taken, b, c = [], 0, 0
            while len(taken) < line - 1:
                if c < above and (c <= b or b >= below):
                    c += 1
                    taken.append((c, a + c))
                else:
                    b += 1
                    taken.append((-b, a - b))
            order.append(taken)
        for rank in range(line - 1):
            choices = sorted({order[a][rank][0] for a in range(line)})
            value, source = None, 0
            for choice in choices:
                levels = [a for a in range(line) if order[a][rank][0] == choice]
                arrived = downs[choice] if choice > 0 else ups[-choice]
                here = jnp.zeros((), bool)
                for a in levels:
                    here = here | (level == a)
                value = arrived if value is None else jnp.where(here, arrived, value)
            for a in range(line):
                source = jnp.where(level == a, order[a][rank][1], source)
            found.append((source, value))
        return found

    gram = jnp.zeros((line, 2, count, total), jnp.bfloat16)
    images = [jnp.zeros((line, 2, count, slab), jnp.bfloat16) for _ in range(row_devices)]
    for part in range(2):
        found = spread(reduced(gram_parts[part]))
        for first in range(0, line, 2):
            group = found[first:first + 2]
            rows = []
            for source, value in group:
                both = [value, swap(value)]
                rows += both
                for side, block in zip((core, 1 - core), both):
                    gram = lax.dynamic_update_slice(
                        gram, block[None, None], (source, side, part * half, 0)
                    )
            image = jnp.dot(
                jnp.concatenate(rows), near, preferred_element_type=jnp.float32
            ).astype(jnp.bfloat16)
            for distance, block in enumerate(square(image)):
                block = block.reshape(len(group), 2, half, slab)
                for index, (source, _) in enumerate(group):
                    for side in range(2):
                        images[distance] = lax.dynamic_update_slice(
                            images[distance],
                            block[index, side][None, None],
                            (source, core if side == 0 else 1 - core, part * half, 0),
                        )
    gram = gram.reshape(2 * line * count, total)
    images = [block.reshape(2 * line * count, slab) for block in images]
    second = jnp.dot(gram, jnp.concatenate(images), preferred_element_type=jnp.float32)
    return combine(near[: 2 * line * count], images[0], second, gain)


def solution(mesh):
    square_of_lines = mesh.shape["row"] == 4 and mesh.shape["col"] in (4, 6, 8)

    def program(iterate):
        gain = output_gain * math.sqrt(max(iterate.shape))
        plan = neighbour_plan if square_of_lines else gathered_plan
        return jax.shard_map(
            lambda block: plan(block, gain),
            mesh=mesh,
            in_specs=(P(("row", "col"), None),),
            out_specs=P("row", "col"),
            check_vma=False,
        )(iterate)

    return program
```

```python
import functools
import math

import jax
import jax.numpy as jnp
from jax import lax
from jax.experimental import pallas as pl
from jax.experimental.pallas import tpu as pltpu
from jax.sharding import PartitionSpec as P

linear_weight = 3.4445
cubic_weight = -4.775
quintic_weight = 2.0315
output_gain = 0.2


def gather_rows(block_rows):
    return lax.all_gather(block_rows, "row", axis=0, tiled=True)


def strided_order(panel_rows, row_devices, col_devices):
    total_rows, column_count = panel_rows.shape
    per_device = total_rows // (row_devices * col_devices)
    grouped = panel_rows.reshape(row_devices, col_devices, per_device, column_count)
    return jnp.transpose(grouped, (1, 0, 2, 3)).reshape(total_rows, column_count)


def row_product(left_rows, right_rows):
    return lax.dot_general(
        left_rows, right_rows, (((1,), (1,)), ((), ())), preferred_element_type=jnp.float32
    )


def combine(scaled_tile, image_tile, second_term, gain):
    combined = (
        linear_weight * scaled_tile.astype(jnp.float32)
        + cubic_weight * image_tile.astype(jnp.float32)
        + quintic_weight * second_term
    )
    return (gain * combined).astype(jnp.bfloat16)


def gathered_plan(iterate, gain):
    scaled_tile = lax.all_to_all(iterate, "col", split_axis=1, concat_axis=0, tiled=True)
    row_devices = lax.axis_size("row")
    col_devices = lax.axis_size("col")
    strided_rows = gather_rows(iterate)
    panel_rows = lax.all_gather(scaled_tile, "col", axis=1, tiled=True)
    gram_tile = row_product(panel_rows, strided_rows).astype(jnp.bfloat16)
    gram_wide = lax.all_gather(gram_tile, "col", axis=1, tiled=True)
    scaled_columns = strided_order(gather_rows(scaled_tile), row_devices, col_devices)
    image_tile = jnp.dot(gram_wide, scaled_columns, preferred_element_type=jnp.float32).astype(
        jnp.bfloat16
    )
    image_columns = strided_order(gather_rows(image_tile), row_devices, col_devices)
    second_term = jnp.dot(gram_wide, image_columns, preferred_element_type=jnp.float32)
    return combine(scaled_tile, image_tile, second_term, gain)


def call(
    kernel, out_shape, operands, flops, scratch=(), space=pltpu.VMEM, out_space=pltpu.VMEM
):
    specs = [pl.BlockSpec(memory_space=pltpu.SMEM)]
    specs += [pl.BlockSpec(memory_space=space)] * (len(operands) - 1)
    moved = sum(math.prod(v.shape) * v.dtype.itemsize for v in operands)
    return pl.pallas_call(
        kernel,
        in_specs=specs,
        out_specs=pl.BlockSpec(memory_space=out_space),
        out_shape=out_shape,
        scratch_shapes=list(scratch),
        compiler_params=pltpu.CompilerParams(vmem_limit_bytes=48 * 1024 * 1024),
        cost_estimate=pl.CostEstimate(flops=flops, bytes_accessed=moved, transcendentals=0),
    )(*operands)


def matmul(left, right):
    return jnp.dot(left, right, preferred_element_type=jnp.float32)


def taken_core(meta_ref, e, distance):
    return meta_ref[3] ^ (e >> 1) if distance == 2 else meta_ref[2] ^ (e & 1)


def level_of(meta_ref, slot, line):
    return lax.rem(meta_ref[0] + slot, line)


def place_pieces(held_ref, refs, levels):
    half = refs[3].shape[0]
    for i, level in enumerate(levels):
        for e in range(3):
            held_ref[e, level] = refs[5 * i + e][...]
        held_ref[3, level, :half] = refs[5 * i + 3][...]
        held_ref[3, level, half:] = refs[5 * i + 4][...]


def own_blocks_kernel(line, meta_ref, *refs):
    out_ref, mine_ref, pair_ref = refs[-3:]
    count, depth = mine_ref.shape[1:]
    size = line * count
    for i in range(line):
        level = level_of(meta_ref, i, line)
        mine_ref[level] = refs[i][...]
        pair_ref[level] = refs[line + i][...]

    def step(i, carry):
        left = mine_ref[pl.ds(2 * i, 2)].reshape(2 * count, depth)
        for index, right_ref in enumerate((mine_ref, pair_ref)):
            product = row_product(left, right_ref[...].reshape(size, depth))
            out_ref[pl.ds(2 * i, 2), :, index * size:(index + 1) * size] = product.astype(
                out_ref.dtype
            ).reshape(2, count, size)
        return carry

    lax.fori_loop(0, line // 2, step, 0)


def cross_blocks_kernel(line, distances, meta_ref, *refs):
    out_ref, mine_ref, right_ref = refs[-3:]
    count, depth = mine_ref.shape[1:]
    size = line * count
    half = count // 2
    levels = [level_of(meta_ref, i, line) for i in range(line)]
    own = refs[:line]
    pieces = 2 if distances == (3,) else 1
    step_refs = 2 * pieces * len(distances)
    for i in range(line):
        mine_ref[levels[i]] = own[i][...]
    for index, d in enumerate(distances):
        for core in range(2):

            @pl.when(taken_core(meta_ref, 0, d) == core)
            def _():
                for i in range(line):
                    first = line + step_refs * i + 2 * pieces * index + pieces * core
                    if pieces == 1:
                        right_ref[levels[i]] = refs[first][...]
                    else:
                        right_ref[levels[i], :half] = refs[first][...]
                        right_ref[levels[i], half:] = refs[first + 1][...]

        def step(i, carry):
            left = mine_ref[pl.ds(2 * i, 2)].reshape(2 * count, depth)
            product = row_product(left, right_ref[...].reshape(size, depth))
            out_ref[pl.ds(2 * i, 2), :, index * size:(index + 1) * size] = product.astype(
                out_ref.dtype
            ).reshape(2, count, size)
            return carry

        lax.fori_loop(0, line // 2, step, 0)


def columns_kernel(line, slab, meta_ref, *refs):
    out_ref, held_ref = refs[-2:]
    count = held_ref.shape[2]
    levels = [level_of(meta_ref, i, line) for i in range(line)]
    columns = pl.ds(pl.multiple_of(meta_ref[1] * slab, slab), slab)
    for i in range(line):
        for k in range(2):
            group = refs[10 * i + 5 * k:10 * i + 5 * k + 5]
            for e in range(3):
                held_ref[2 * e + k, levels[i]] = group[e][:, columns]
            held_ref[6 + k, levels[i], :count // 2] = group[3][:, columns]
            held_ref[6 + k, levels[i], count // 2:] = group[4][:, columns]

    def step(i, carry):
        group, level = i // line, lax.rem(i, line)
        out_ref[group // 2, lax.rem(group, 2), level] = held_ref[group, level].T
        return carry

    lax.fori_loop(0, 8 * line, step, 0)


def met_places(meta_ref, e, k):
    return [(e, k), (e, 1 - k)] + [(e ^ d, k ^ taken_core(meta_ref, e, d)) for d in (1, 2, 3)]


def side_by_side(turned_ref, places):
    line = turned_ref.shape[2]
    return jnp.concatenate(
        [turned_ref[a, b, level] for a, b in places for level in range(line)], axis=1
    )


def start_all(copies):
    for copy in copies:
        copy.start()
    return copies


def wait_all(copies):
    for copy in copies:
        copy.wait()


def shard_copies(refs, held_ref, sems):
    half = held_ref.shape[3] // 2
    copies = []
    for i in range(held_ref.shape[2]):
        for k in range(2):
            group = refs[10 * i + 5 * k:10 * i + 5 * k + 5]
            targets = [held_ref.at[e, k, i] for e in range(3)]
            targets += [held_ref.at[3, k, i, :half], held_ref.at[3, k, i, half:]]
            for source, target in zip(group, targets):
                copies.append(pltpu.make_async_copy(source, target, sems.at[len(copies)]))
    return copies


def image_parts(meta_ref, xt_ref, held_ref, levels, e, k):
    line, width, count = xt_ref.shape[2:]
    size = line * count
    slots = len(levels)
    left, right = [], []
    for d in (1, 2, 3):
        a = e ^ d
        b = k ^ taken_core(meta_ref, a, d)
        for n in range(slots):
            left.append(xt_ref[a, b, levels[n]])
            right.append(held_ref[a, b, n, :, (1 + d) * size:(2 + d) * size])
    back = matmul(jnp.concatenate(left, axis=1), jnp.concatenate(right))
    forth = row_product(
        side_by_side(xt_ref, met_places(meta_ref, e, k)),
        held_ref[e, k].reshape(slots * count, 5 * size),
    )
    return back, forth


def early_kernel(slots, meta_ref, xt_hbm, *refs):
    acc_hbm, xt_ref, held_ref, acc_ref, sems, out_sems = refs[-6:]
    line, width, count = xt_ref.shape[2:]
    levels = [level_of(meta_ref, i, line) for i in range(slots)]
    copies = shard_copies(refs, held_ref, sems)
    copies.append(pltpu.make_async_copy(xt_hbm, xt_ref, sems.at[len(copies)]))
    wait_all(start_all(copies))

    def out_copy(i):
        return pltpu.make_async_copy(
            acc_ref.at[i // 2, lax.rem(i, 2)], acc_hbm.at[i // 2, lax.rem(i, 2)], out_sems.at[i]
        )

    def step(i, carry):
        e, k = i // 2, lax.rem(i, 2)
        back, forth = image_parts(meta_ref, xt_ref, held_ref, levels, e, k)
        for level in range(line):
            acc_ref[e, k, level] = back[:, level * count:(level + 1) * count]
        for n in range(slots):
            acc_ref[e, k, levels[n]] += forth[:, n * count:(n + 1) * count]
        out_copy(i).start()
        return carry

    lax.fori_loop(0, 8, step, 0)
    for i in range(8):
        out_copy(i).wait()


def last_kernel(gain, slots, meta_ref, xt_hbm, acc_hbm, *refs):
    out_ref, xt_ref, held_ref, acc_ref, image_ref, own_ref, cross_ref, back_ref = refs[-11:-3]
    sems, acc_sems, later_sems = refs[-3:]
    line, width, count = xt_ref.shape[2:]
    size = line * count
    half = count // 2
    slot_levels = [level_of(meta_ref, i, line) for i in range(line)]
    levels = slot_levels[line - slots:]
    copies = shard_copies(refs[10 * (line - slots):10 * line], held_ref, sems)
    copies.append(pltpu.make_async_copy(xt_hbm, xt_ref, sems.at[len(copies)]))
    start_all(copies)

    def acc_copy(i):
        held = lax.rem(i, 2)
        return pltpu.make_async_copy(
            acc_hbm.at[i // 2, held], acc_ref.at[held], acc_sems.at[held]
        )

    for i in range(2):
        acc_copy(i).start()
    later = []
    for i in range(line):
        for k in range(2):
            group = refs[10 * i + 5 * k:10 * i + 5 * k + 5]
            parts = [(group[0], own_ref.at[k, i])]
            for d in (1, 2):
                columns = pl.ds((1 + d) * size, size)
                parts.append((group[d].at[:, columns], cross_ref.at[d - 1, k, i]))
            columns = pl.ds(4 * size, size)
            parts.append((group[3].at[:, columns], cross_ref.at[2, k, i, :half]))
            parts.append((group[4].at[:, columns], cross_ref.at[2, k, i, half:]))
            for source, target in parts:
                later.append(pltpu.make_async_copy(source, target, later_sems.at[len(later)]))
    start_all(later)
    wait_all(copies)

    def step(i, carry):
        e, k = i // 2, lax.rem(i, 2)
        back, forth = image_parts(meta_ref, xt_ref, held_ref, levels, e, k)
        acc_copy(i).wait()
        for n in range(slots):
            acc_ref[k, levels[n]] += forth[:, n * count:(n + 1) * count]
        for level in range(line):
            total = acc_ref[k, level] + back[:, level * count:(level + 1) * count]
            image_ref[e, k, level] = total.astype(jnp.bfloat16)

        @pl.when(i < 6)
        def _():
            acc_copy(i + 2).start()

        return carry

    lax.fori_loop(0, 8, step, 0)
    wait_all(later)

    def finish(k, carry):
        places = [(d, k ^ taken_core(meta_ref, d, d)) for d in (1, 2, 3)]
        blocks = [cross_ref[d - 1, b].reshape(size, size) for d, b in places]
        rows = [image_ref[d, b, level] for d, b in places for level in slot_levels]
        back = matmul(jnp.concatenate(rows, axis=1), jnp.concatenate(blocks))
        for level in range(line):
            back_ref[level] = back[:, level * count:(level + 1) * count]
        forth = row_product(
            side_by_side(image_ref, met_places(meta_ref, 0, k)),
            own_ref[k].reshape(size, 5 * size),
        )
        core = meta_ref[1] ^ k
        for i, level in enumerate(slot_levels):
            second = forth[:, i * count:(i + 1) * count] + back_ref[level]
            turned = combine(xt_ref[0, k, level], image_ref[0, k, level], second, gain)
            out_ref[level, core] = turned.T
        return carry

    lax.fori_loop(0, 2, finish, 0)


def after(values, *others):
    return lax.optimization_barrier((values,) + others)[0]


def neighbour_plan(iterate, gain):
    line = lax.axis_size("col") // 2
    count, width = iterate.shape
    slab = width // (2 * line)
    size = line * count
    row_devices = lax.axis_size("row")
    place, row = lax.axis_index("col"), lax.axis_index("row")
    level, core = place // 2, place % 2
    meta = jnp.stack([level, core, row & 1, row >> 1]).astype(jnp.int32)

    def along(values, hop):
        pairs = [(2 * a + k, 2 * ((a - hop) % line) + k) for a in range(line) for k in range(2)]
        return lax.ppermute(values, "col", pairs)

    def swap(values):
        pairs = [(2 * a + k, 2 * a + 1 - k) for a in range(line) for k in range(2)]
        return lax.ppermute(values, "col", pairs)

    def across(values, bit):
        return lax.ppermute(values, "row", [(i, i ^ bit) for i in range(row_devices)])

    pieces, last = [None] * line, None
    for hop in sorted(range(line), key=lambda h: min(h, line - h)):
        start = ((level - hop) % line) * (2 * slab)
        piece = lax.dynamic_slice(iterate, (0, start), (count, 2 * slab))
        if hop:
            piece = after(piece, last) if 1 < hop < line - 1 else piece
            piece = along(piece, hop)
            last = piece if last is None else last
        pieces[hop] = piece
    flops = 4 * size * size * slab
    held = [pltpu.VMEM((line, count, 2 * slab), jnp.bfloat16)] * 2

    def summed(partial, *others):
        chunks = [
            along(lax.dynamic_index_in_dim(partial, (level - hop) % line, 0, False), hop)
            for hop in range(1, line)
        ]
        if others:
            chunks[0] = after(chunks[0], *others)
        total = lax.dynamic_index_in_dim(partial, level, 0, False).astype(jnp.float32)
        for chunk in chunks:
            total += chunk.astype(jnp.float32)
        return total.astype(jnp.bfloat16)

    own_swapped = [swap(piece) for piece in pieces]
    own_blocks = call(
        functools.partial(own_blocks_kernel, line),
        jax.ShapeDtypeStruct((line, count, 2 * size), jnp.bfloat16),
        [meta] + pieces + own_swapped,
        2 * flops,
        scratch=held,
    )
    own_shard = summed(own_blocks)

    half = count // 2
    x_slots = []
    for index, piece in enumerate(pieces):
        one, two = across(piece, 1), across(piece, 2)
        x_slots.append([piece, one, two, None, None, own_swapped[index], swap(one), swap(two)])
    side_blocks = call(
        functools.partial(cross_blocks_kernel, line, (1, 2)),
        jax.ShapeDtypeStruct((line, count, 2 * size), jnp.bfloat16),
        [meta] + pieces + [v for slot in x_slots for v in (slot[1], slot[6], slot[2], slot[7])],
        2 * flops,
        scratch=held,
    )
    for index, slot in enumerate(x_slots):
        one, two = slot[1], slot[2]
        if 1 < index < line - 1:
            one, two = after(one, own_blocks), after(two, own_blocks)
        slot[3], slot[4] = across(one[:half], 2), across(two[half:], 1)
        slot += [swap(slot[3]), swap(slot[4])]
    corner_blocks = call(
        functools.partial(cross_blocks_kernel, line, (3,)),
        jax.ShapeDtypeStruct((line, count, size), jnp.bfloat16),
        [meta] + pieces + [v for slot in x_slots for v in (slot[3], slot[4], slot[8], slot[9])],
        flops,
        scratch=held,
    )
    side_shard = summed(side_blocks)
    xt = call(
        functools.partial(columns_kernel, line, slab),
        jax.ShapeDtypeStruct((4, 2, line, slab, count), jnp.bfloat16),
        [meta] + [v for slot in x_slots for v in slot],
        size * slab * 512,
        scratch=[pltpu.VMEM((8, line, count, slab), jnp.bfloat16)],
    )
    corner_shard = summed(corner_blocks, xt)
    shard = jnp.concatenate([own_shard, side_shard, corner_shard], axis=1)

    cut = line // 2
    shards = [shard]
    for hop in range(1, line):
        shards.append(along(shards[-1], 1))
    slots, acc = [], None
    for first in range(0, line, cut):
        group = []
        for shard in shards[first:first + cut]:
            group.append((shard, across(shard, 1), across(shard, 2)))
        for shard, one, two in group:
            if acc is not None:
                one, two = after(one, acc), after(two, acc)
            blocks = [shard, one, two, across(one[:half], 2), across(two[half:], 1)]
            slots.append(blocks + [swap(block) for block in blocks])
        if acc is not None:
            break
        acc = call(
            functools.partial(early_kernel, cut),
            jax.ShapeDtypeStruct(xt.shape, jnp.float32),
            [meta, xt] + [v for slot in slots for v in slot],
            128 * cut * count * size * slab,
            scratch=[
                pltpu.VMEM(xt.shape, jnp.bfloat16),
                pltpu.VMEM((4, 2, cut, count, 5 * size), jnp.bfloat16),
                pltpu.VMEM(xt.shape, jnp.float32),
                pltpu.SemaphoreType.DMA((10 * cut + 1,)),
                pltpu.SemaphoreType.DMA((8,)),
            ],
            space=pl.ANY,
            out_space=pl.ANY,
        )
    update = call(
        functools.partial(last_kernel, gain, line - cut),
        jax.ShapeDtypeStruct((line, 2, count, slab), jnp.bfloat16),
        [meta, xt, acc] + [v for slot in slots for v in slot],
        (128 * (line - cut) * count + 32 * size) * size * slab,
        scratch=[
            pltpu.VMEM(xt.shape, jnp.bfloat16),
            pltpu.VMEM((4, 2, line - cut, count, 5 * size), jnp.bfloat16),
            pltpu.VMEM((2, line, slab, count), jnp.float32),
            pltpu.VMEM(xt.shape, jnp.bfloat16),
            pltpu.VMEM((2, line, count, 5 * size), jnp.bfloat16),
            pltpu.VMEM((3, 2, line, count, size), jnp.bfloat16),
            pltpu.VMEM((line, slab, count), jnp.float32),
            pltpu.SemaphoreType.DMA((10 * (line - cut) + 1,)),
            pltpu.SemaphoreType.DMA((2,)),
            pltpu.SemaphoreType.DMA((10 * line,)),
        ],
        space=pl.ANY,
    )
    return update.reshape(2 * size, slab)


def solution(mesh):
    square_of_lines = mesh.shape["row"] == 4 and mesh.shape["col"] in (4, 6, 8)

    def program(iterate):
        gain = output_gain * math.sqrt(max(iterate.shape))
        plan = neighbour_plan if square_of_lines else gathered_plan
        return jax.shard_map(
            lambda block: plan(block, gain),
            mesh=mesh,
            in_specs=(P(("row", "col"), None),),
            out_specs=P("row", "col"),
            check_vma=False,
        )(iterate)

    return program
```

```python
import functools
import math

import jax
import jax.numpy as jnp
from jax import lax
from jax.experimental import pallas as pl
from jax.experimental.pallas import tpu as pltpu
from jax.sharding import PartitionSpec as P

linear_weight = 3.4445
cubic_weight = -4.775
quintic_weight = 2.0315
output_gain = 0.2


def gather_rows(block_rows):
    return lax.all_gather(block_rows, "row", axis=0, tiled=True)


def strided_order(panel_rows, row_devices, col_devices):
    total_rows, column_count = panel_rows.shape
    per_device = total_rows // (row_devices * col_devices)
    grouped = panel_rows.reshape(row_devices, col_devices, per_device, column_count)
    return jnp.transpose(grouped, (1, 0, 2, 3)).reshape(total_rows, column_count)


def row_product(left_rows, right_rows):
    return lax.dot_general(
        left_rows, right_rows, (((1,), (1,)), ((), ())), preferred_element_type=jnp.float32
    )


def combine(scaled_tile, image_tile, second_term, gain):
    combined = (
        linear_weight * scaled_tile.astype(jnp.float32)
        + cubic_weight * image_tile.astype(jnp.float32)
        + quintic_weight * second_term
    )
    return (gain * combined).astype(jnp.bfloat16)


def gathered_plan(iterate, gain):
    scaled_tile = lax.all_to_all(iterate, "col", split_axis=1, concat_axis=0, tiled=True)
    row_devices = lax.axis_size("row")
    col_devices = lax.axis_size("col")
    strided_rows = gather_rows(iterate)
    panel_rows = lax.all_gather(scaled_tile, "col", axis=1, tiled=True)
    gram_tile = row_product(panel_rows, strided_rows).astype(jnp.bfloat16)
    gram_wide = lax.all_gather(gram_tile, "col", axis=1, tiled=True)
    scaled_columns = strided_order(gather_rows(scaled_tile), row_devices, col_devices)
    image_tile = jnp.dot(gram_wide, scaled_columns, preferred_element_type=jnp.float32).astype(
        jnp.bfloat16
    )
    image_columns = strided_order(gather_rows(image_tile), row_devices, col_devices)
    second_term = jnp.dot(gram_wide, image_columns, preferred_element_type=jnp.float32)
    return combine(scaled_tile, image_tile, second_term, gain)


def call(
    kernel, out_shape, operands, flops, scratch=(), space=pltpu.VMEM, out_space=pltpu.VMEM
):
    specs = [pl.BlockSpec(memory_space=pltpu.SMEM)]
    specs += [pl.BlockSpec(memory_space=space)] * (len(operands) - 1)
    moved = sum(math.prod(v.shape) * v.dtype.itemsize for v in operands)
    return pl.pallas_call(
        kernel,
        in_specs=specs,
        out_specs=pl.BlockSpec(memory_space=out_space),
        out_shape=out_shape,
        scratch_shapes=list(scratch),
        compiler_params=pltpu.CompilerParams(vmem_limit_bytes=48 * 1024 * 1024),
        cost_estimate=pl.CostEstimate(flops=flops, bytes_accessed=moved, transcendentals=0),
    )(*operands)


def matmul(left, right):
    return jnp.dot(left, right, preferred_element_type=jnp.float32)


def taken_core(meta_ref, e, distance):
    return meta_ref[3] ^ (e >> 1) if distance == 2 else meta_ref[2] ^ (e & 1)


def level_of(meta_ref, slot, line):
    return lax.rem(meta_ref[0] + slot, line)


def place_rows(held_ref, lead, parts, levels, columns=slice(None)):
    half = held_ref.shape[-2] // 2
    done = 0
    for part in parts:
        for start in range(0, part.shape[0], half):
            slot, place = divmod(done + start, 2 * half)
            to = lead + (levels[slot], slice(place, place + half))
            held_ref[to] = part[start:start + half, columns]
        done += part.shape[0]


def left_products(mine_ref, right, out_ref, index):
    line, count, depth = mine_ref.shape
    size = line * count

    def step(i, carry):
        left = mine_ref[pl.ds(2 * i, 2)].reshape(2 * count, depth)
        product = row_product(left, right[...].reshape(size, depth))
        out_ref[pl.ds(2 * i, 2), :, index * size:(index + 1) * size] = product.astype(
            out_ref.dtype
        ).reshape(2, count, size)
        return carry

    lax.fori_loop(0, line // 2, step, 0)


def own_blocks_kernel(meta_ref, *refs):
    out_ref, mine_ref, pair_ref = refs[-3:]
    line = mine_ref.shape[0]
    levels = [level_of(meta_ref, i, line) for i in range(line)]
    place_rows(mine_ref, (), refs[:1], levels)
    place_rows(pair_ref, (), refs[1:2], levels)
    left_products(mine_ref, mine_ref, out_ref, 0)
    left_products(mine_ref, pair_ref, out_ref, 1)


def group_of(meta_ref, k, order):
    core = meta_ref[1] ^ k
    return (0, 1 + core, 2 - core, 3)[order]


def side_blocks_kernel(meta_ref, *refs):
    out_ref, mine_ref, right_ref = refs[-3:]
    line = mine_ref.shape[0]
    levels = [level_of(meta_ref, i, line) for i in range(line)]
    place_rows(mine_ref, (), refs[:1], levels)
    for d in (1, 2):
        for k in range(2):
            for order in (1, 2):
                is_core = taken_core(meta_ref, 0, d) == k

                @pl.when(jnp.logical_and(is_core, group_of(meta_ref, k, order) == d))
                def _():
                    place_rows(right_ref, (), [refs[2 * k + order]], levels)

        left_products(mine_ref, right_ref, out_ref, d - 1)


def corner_blocks_kernel(meta_ref, *refs):
    out_ref, mine_ref, right_ref = refs[-3:]
    line = mine_ref.shape[0]
    levels = [level_of(meta_ref, i, line) for i in range(line)]
    place_rows(mine_ref, (), refs[:1], levels)
    for k in range(2):

        @pl.when(taken_core(meta_ref, 0, 3) == k)
        def _():
            place_rows(right_ref, (), [refs[1 + k]], levels)

    left_products(mine_ref, right_ref, out_ref, 0)


def columns_kernel(slab, orders, meta_ref, *refs):
    out_ref, held_ref = refs[-2:]
    groups, _, line = held_ref.shape[:3]
    levels = [level_of(meta_ref, i, line) for i in range(line)]
    columns = pl.ds(pl.multiple_of(meta_ref[1] * slab, slab), slab)
    for k in range(2):
        for index, order in enumerate(orders):
            e = group_of(meta_ref, k, order) - orders[0]
            place_rows(held_ref, (e, k), [refs[len(orders) * k + index]], levels, columns)

    def step(i, carry):
        group, level = i // line, lax.rem(i, line)
        e, k = group // 2, lax.rem(group, 2)
        out_ref[e, k, level] = held_ref[e, k, level].T
        return carry

    lax.fori_loop(0, 2 * groups * line, step, 0)


def met_places(meta_ref, e, k):
    return [(e, k), (e, 1 - k)] + [(e ^ d, k ^ taken_core(meta_ref, e, d)) for d in (1, 2, 3)]


def side_by_side(turned_ref, places):
    line = turned_ref.shape[2]
    return jnp.concatenate(
        [turned_ref[a, b, level] for a, b in places for level in range(line)], axis=1
    )


def start_all(copies):
    for copy in copies:
        copy.start()
    return copies


def wait_all(copies):
    for copy in copies:
        copy.wait()


def shard_copies(meta_ref, refs, slots, held_ref, sems):
    copies = []
    for i, slot in enumerate(slots):
        for k in range(2):
            for order in range(4):
                source = refs[8 * slot + 4 * k + order]
                target = held_ref.at[group_of(meta_ref, k, order), k, i]
                copies.append(pltpu.make_async_copy(source, target, sems.at[len(copies)]))
    return copies


def column_copies(near_hbm, far_hbm, xt_ref, sems, used):
    parts = ((near_hbm, xt_ref.at[:3]), (far_hbm, xt_ref.at[3:]))
    return [
        pltpu.make_async_copy(source, target, sems.at[used + i])
        for i, (source, target) in enumerate(parts)
    ]


def image_parts(meta_ref, xt_ref, held_ref, levels, e, k):
    line, width, count = xt_ref.shape[2:]
    size = line * count
    slots = len(levels)
    left, right = [], []
    for d in (1, 2, 3):
        a = e ^ d
        b = k ^ taken_core(meta_ref, a, d)
        for n in range(slots):
            left.append(xt_ref[a, b, levels[n]])
            right.append(held_ref[a, b, n, :, (1 + d) * size:(2 + d) * size])
    back = matmul(jnp.concatenate(left, axis=1), jnp.concatenate(right))
    forth = row_product(
        side_by_side(xt_ref, met_places(meta_ref, e, k)),
        held_ref[e, k].reshape(slots * count, 5 * size),
    )
    return back, forth


def early_kernel(slots, meta_ref, near_hbm, far_hbm, *refs):
    acc_hbm, xt_ref, held_ref, acc_ref, sems, out_sems = refs[-6:]
    line, width, count = xt_ref.shape[2:]
    levels = [level_of(meta_ref, i, line) for i in range(slots)]
    copies = shard_copies(meta_ref, refs, range(slots), held_ref, sems)
    copies += column_copies(near_hbm, far_hbm, xt_ref, sems, len(copies))
    wait_all(start_all(copies))

    def out_copy(i):
        return pltpu.make_async_copy(
            acc_ref.at[i // 2, lax.rem(i, 2)], acc_hbm.at[i // 2, lax.rem(i, 2)], out_sems.at[i]
        )

    def step(i, carry):
        e, k = i // 2, lax.rem(i, 2)
        back, forth = image_parts(meta_ref, xt_ref, held_ref, levels, e, k)
        for level in range(line):
            acc_ref[e, k, level] = back[:, level * count:(level + 1) * count]
        for n in range(slots):
            acc_ref[e, k, levels[n]] += forth[:, n * count:(n + 1) * count]
        out_copy(i).start()
        return carry

    lax.fori_loop(0, 8, step, 0)
    for i in range(8):
        out_copy(i).wait()


def last_kernel(gain, slots, meta_ref, near_hbm, far_hbm, acc_hbm, *refs):
    out_ref, xt_ref, held_ref, acc_ref, image_ref, own_ref, cross_ref, back_ref = refs[-11:-3]
    sems, acc_sems, later_sems = refs[-3:]
    line, width, count = xt_ref.shape[2:]
    size = line * count
    slot_levels = [level_of(meta_ref, i, line) for i in range(line)]
    levels = slot_levels[line - slots:]
    copies = shard_copies(meta_ref, refs, range(line - slots, line), held_ref, sems)
    copies += column_copies(near_hbm, far_hbm, xt_ref, sems, len(copies))
    start_all(copies)

    def acc_copy(i):
        held = lax.rem(i, 2)
        return pltpu.make_async_copy(
            acc_hbm.at[i // 2, held], acc_ref.at[held], acc_sems.at[held]
        )

    for i in range(2):
        acc_copy(i).start()
    later = []
    for i in range(line):
        for k in range(2):
            for order in range(4):
                source, target = refs[8 * i + 4 * k + order], own_ref.at[k, i]
                if order:
                    e = group_of(meta_ref, k, order)
                    first = (1 + e) * size
                    first = pl.multiple_of(first, size) if order < 3 else first
                    source, target = source.at[:, pl.ds(first, size)], cross_ref.at[e - 1, k, i]
                later.append(pltpu.make_async_copy(source, target, later_sems.at[len(later)]))
    start_all(later)
    wait_all(copies)

    def step(i, carry):
        e, k = i // 2, lax.rem(i, 2)
        back, forth = image_parts(meta_ref, xt_ref, held_ref, levels, e, k)
        acc_copy(i).wait()
        for n in range(slots):
            acc_ref[k, levels[n]] += forth[:, n * count:(n + 1) * count]
        for level in range(line):
            total = acc_ref[k, level] + back[:, level * count:(level + 1) * count]
            image_ref[e, k, level] = total.astype(jnp.bfloat16)

        @pl.when(i < 6)
        def _():
            acc_copy(i + 2).start()

        return carry

    lax.fori_loop(0, 8, step, 0)
    wait_all(later)

    def finish(k, carry):
        places = [(d, k ^ taken_core(meta_ref, d, d)) for d in (1, 2, 3)]
        blocks = [cross_ref[d - 1, b].reshape(size, size) for d, b in places]
        rows = [image_ref[d, b, level] for d, b in places for level in slot_levels]
        back = matmul(jnp.concatenate(rows, axis=1), jnp.concatenate(blocks))
        for level in range(line):
            back_ref[level] = back[:, level * count:(level + 1) * count]
        forth = row_product(
            side_by_side(image_ref, met_places(meta_ref, 0, k)),
            own_ref[k].reshape(size, 5 * size),
        )
        core = meta_ref[1] ^ k
        for i, level in enumerate(slot_levels):
            second = forth[:, i * count:(i + 1) * count] + back_ref[level]
            turned = combine(xt_ref[0, k, level], image_ref[0, k, level], second, gain)
            out_ref[level, core] = turned.T
        return carry

    lax.fori_loop(0, 2, finish, 0)


def after(values, *others):
    return lax.optimization_barrier((values,) + others)[0]


def neighbour_plan(iterate, gain):
    line = lax.axis_size("col") // 2
    count, width = iterate.shape
    slab = width // (2 * line)
    size = line * count
    row_devices = lax.axis_size("row")
    place, row = lax.axis_index("col"), lax.axis_index("row")
    level, core = place // 2, place % 2
    meta = jnp.stack([level, core, row & 1, row >> 1]).astype(jnp.int32)

    def along(values, hop):
        pairs = [(2 * a + k, 2 * ((a - hop) % line) + k) for a in range(line) for k in range(2)]
        return lax.ppermute(values, "col", pairs)

    def swap(values):
        pairs = [(2 * a + k, 2 * a + 1 - k) for a in range(line) for k in range(2)]
        return lax.ppermute(values, "col", pairs)

    def across(values, turn):
        pairs = [
            (r * 2 * line + c, (r ^ (1 + (c + turn) % 2)) * 2 * line + c)
            for r in range(row_devices)
            for c in range(2 * line)
        ]
        return lax.ppermute(values, ("row", "col"), pairs)

    def sent(partial):
        return [
            along(lax.dynamic_index_in_dim(partial, (level - hop) % line, 0, False), hop)
            for hop in range(1, line)
        ]

    def summed(partial, chunks):
        total = lax.dynamic_index_in_dim(partial, level, 0, False).astype(jnp.float32)
        for chunk in chunks:
            total += chunk.astype(jnp.float32)
        return total.astype(jnp.bfloat16)

    def piece(hop):
        start = ((level - hop) % line) * (2 * slab)
        return lax.dynamic_slice(iterate, (0, start), (count, 2 * slab))

    tower = jnp.concatenate(
        [along(piece(hop), hop) if hop else piece(0) for hop in range(line)]
    )
    pair_tower = swap(tower)
    flops = 4 * size * size * slab
    held = [pltpu.VMEM((line, count, 2 * slab), jnp.bfloat16)] * 2
    own_blocks = call(
        own_blocks_kernel,
        jax.ShapeDtypeStruct((line, count, 2 * size), jnp.bfloat16),
        [meta, tower, pair_tower],
        2 * flops,
        scratch=held,
    )
    own_shard = summed(own_blocks, sent(own_blocks))
    one, two = after(across(tower, 0), own_shard), after(across(tower, 1), own_shard)
    pair_one, pair_two = swap(one), swap(two)
    side_blocks = call(
        side_blocks_kernel,
        jax.ShapeDtypeStruct((line, count, 2 * size), jnp.bfloat16),
        [meta, tower, one, two, pair_one, pair_two],
        2 * flops,
        scratch=held,
    )
    def columns(orders, *blocks):
        return call(
            functools.partial(columns_kernel, slab, orders),
            jax.ShapeDtypeStruct((len(orders), 2, line, slab, count), jnp.bfloat16),
            [meta] + list(blocks),
            size * slab * 128 * len(orders),
            scratch=[pltpu.VMEM((len(orders), 2, line, count, slab), jnp.bfloat16)],
        )

    side_sent = sent(side_blocks)
    near_columns = columns((0, 1, 2), tower, one, two, pair_tower, pair_one, pair_two)
    three = after(across(one, 1), side_sent[0], side_sent[-1], near_columns)
    pair_three = swap(three)
    corner_blocks = call(
        corner_blocks_kernel,
        jax.ShapeDtypeStruct((line, count, size), jnp.bfloat16),
        [meta, tower, three, pair_three],
        flops,
        scratch=held,
    )
    far_columns = columns((3,), three, pair_three)
    side_shard = summed(side_blocks, side_sent)
    corner_shard = summed(corner_blocks, sent(corner_blocks))
    shard = jnp.concatenate([own_shard, side_shard, corner_shard], axis=1)

    cut = line // 2
    turned = (4, 2, line, slab, count)
    near, ring, one, two, three = [shard], [], [], [], []

    def pieces(slots):
        own = [[near[i], one[i], two[i], three[i]] for i in slots]
        return [v for blocks in own for v in blocks + [swap(block) for block in blocks]]

    def early():
        return call(
            functools.partial(early_kernel, cut),
            jax.ShapeDtypeStruct(turned, jnp.float32),
            [meta, near_columns, far_columns] + pieces(range(cut)),
            128 * cut * count * size * slab,
            scratch=[
                pltpu.VMEM(turned, jnp.bfloat16),
                pltpu.VMEM((4, 2, cut, count, 5 * size), jnp.bfloat16),
                pltpu.VMEM(turned, jnp.float32),
                pltpu.SemaphoreType.DMA((8 * cut + 2,)),
                pltpu.SemaphoreType.DMA((8,)),
            ],
            space=pl.ANY,
            out_space=pl.ANY,
        )

    for step in range(line + 1):
        done = [blocks[-1] for blocks in (ring, one, two, three) if blocks]
        if step == line:
            acc = early()
            done.append(acc)
        if step:
            three.append(across(after(one[-1], *done), 1))
        if step < line:
            here = after(near[step], *done) if step else near[0]
            one.append(across(here, 0))
            two.append(across(here, 1))
        if step < line - 1:
            ring.append(along(here, 1))
            near.append(ring[-1])
    update = call(
        functools.partial(last_kernel, gain, line - cut),
        jax.ShapeDtypeStruct((line, 2, count, slab), jnp.bfloat16),
        [meta, near_columns, far_columns, acc] + pieces(range(line)),
        (128 * (line - cut) * count + 32 * size) * size * slab,
        scratch=[
            pltpu.VMEM(turned, jnp.bfloat16),
            pltpu.VMEM((4, 2, line - cut, count, 5 * size), jnp.bfloat16),
            pltpu.VMEM((2, line, slab, count), jnp.float32),
            pltpu.VMEM(turned, jnp.bfloat16),
            pltpu.VMEM((2, line, count, 5 * size), jnp.bfloat16),
            pltpu.VMEM((3, 2, line, count, size), jnp.bfloat16),
            pltpu.VMEM((line, slab, count), jnp.float32),
            pltpu.SemaphoreType.DMA((8 * (line - cut) + 2,)),
            pltpu.SemaphoreType.DMA((2,)),
            pltpu.SemaphoreType.DMA((8 * line,)),
        ],
        space=pl.ANY,
    )
    return update.reshape(2 * size, slab)


def solution(mesh):
    square_of_lines = mesh.shape["row"] == 4 and mesh.shape["col"] in (4, 6, 8)

    def program(iterate):
        gain = output_gain * math.sqrt(max(iterate.shape))
        plan = neighbour_plan if square_of_lines else gathered_plan
        return jax.shard_map(
            lambda block: plan(block, gain),
            mesh=mesh,
            in_specs=(P(("row", "col"), None),),
            out_specs=P("row", "col"),
            check_vma=False,
        )(iterate)

    return program
```

```python
import functools
import math

import jax
import jax.numpy as jnp
from jax import lax
from jax.experimental import pallas as pl
from jax.experimental.pallas import tpu as pltpu
from jax.sharding import PartitionSpec as P

linear_weight = 3.4445
cubic_weight = -4.775
quintic_weight = 2.0315
output_gain = 0.2


def gather_rows(block_rows):
    return lax.all_gather(block_rows, "row", axis=0, tiled=True)


def strided_order(panel_rows, row_devices, col_devices):
    total_rows, column_count = panel_rows.shape
    per_device = total_rows // (row_devices * col_devices)
    grouped = panel_rows.reshape(row_devices, col_devices, per_device, column_count)
    return jnp.transpose(grouped, (1, 0, 2, 3)).reshape(total_rows, column_count)


def row_product(left_rows, right_rows):
    return lax.dot_general(
        left_rows, right_rows, (((1,), (1,)), ((), ())), preferred_element_type=jnp.float32
    )


def combine(scaled_tile, image_tile, second_term, gain):
    combined = (
        linear_weight * scaled_tile.astype(jnp.float32)
        + cubic_weight * image_tile.astype(jnp.float32)
        + quintic_weight * second_term
    )
    return (gain * combined).astype(jnp.bfloat16)


def gathered_plan(iterate, gain):
    scaled_tile = lax.all_to_all(iterate, "col", split_axis=1, concat_axis=0, tiled=True)
    row_devices = lax.axis_size("row")
    col_devices = lax.axis_size("col")
    strided_rows = gather_rows(iterate)
    panel_rows = lax.all_gather(scaled_tile, "col", axis=1, tiled=True)
    gram_tile = row_product(panel_rows, strided_rows).astype(jnp.bfloat16)
    gram_wide = lax.all_gather(gram_tile, "col", axis=1, tiled=True)
    scaled_columns = strided_order(gather_rows(scaled_tile), row_devices, col_devices)
    image_tile = jnp.dot(gram_wide, scaled_columns, preferred_element_type=jnp.float32).astype(
        jnp.bfloat16
    )
    image_columns = strided_order(gather_rows(image_tile), row_devices, col_devices)
    second_term = jnp.dot(gram_wide, image_columns, preferred_element_type=jnp.float32)
    return combine(scaled_tile, image_tile, second_term, gain)


def call(
    kernel, out_shape, operands, flops, scratch=(), space=pltpu.VMEM, out_space=pltpu.VMEM
):
    specs = [pl.BlockSpec(memory_space=pltpu.SMEM)]
    specs += [pl.BlockSpec(memory_space=space)] * (len(operands) - 1)
    moved = sum(math.prod(v.shape) * v.dtype.itemsize for v in operands)
    return pl.pallas_call(
        kernel,
        in_specs=specs,
        out_specs=pl.BlockSpec(memory_space=out_space),
        out_shape=out_shape,
        scratch_shapes=list(scratch),
        compiler_params=pltpu.CompilerParams(vmem_limit_bytes=48 * 1024 * 1024),
        cost_estimate=pl.CostEstimate(flops=flops, bytes_accessed=moved, transcendentals=0),
    )(*operands)


def matmul(left, right):
    return jnp.dot(left, right, preferred_element_type=jnp.float32)


def taken_core(meta_ref, e, distance):
    return meta_ref[3] ^ (e >> 1) if distance == 2 else meta_ref[2] ^ (e & 1)


def level_of(meta_ref, slot, line):
    return lax.rem(meta_ref[0] + slot, line)


def place_rows(held_ref, lead, parts, levels, columns=slice(None)):
    half = held_ref.shape[-2] // 2
    done = 0
    for part in parts:
        for start in range(0, part.shape[0], half):
            slot, place = divmod(done + start, 2 * half)
            to = lead + (levels[slot], slice(place, place + half))
            held_ref[to] = part[start:start + half, columns]
        done += part.shape[0]


def left_products(mine_ref, right, out_ref, index):
    line, count, depth = mine_ref.shape
    size = line * count

    def step(i, carry):
        left = mine_ref[pl.ds(2 * i, 2)].reshape(2 * count, depth)
        product = row_product(left, right[...].reshape(size, depth))
        out_ref[pl.ds(2 * i, 2), :, index * size:(index + 1) * size] = product.astype(
            out_ref.dtype
        ).reshape(2, count, size)
        return carry

    lax.fori_loop(0, line // 2, step, 0)


def own_blocks_kernel(meta_ref, *refs):
    out_ref, mine_ref, pair_ref = refs[-3:]
    line = mine_ref.shape[0]
    levels = [level_of(meta_ref, i, line) for i in range(line)]
    place_rows(mine_ref, (), refs[:1], levels)
    place_rows(pair_ref, (), refs[1:2], levels)
    left_products(mine_ref, mine_ref, out_ref, 0)
    left_products(mine_ref, pair_ref, out_ref, 1)


def group_of(meta_ref, k, order):
    core = meta_ref[1] ^ k
    return (0, 1 + core, 2 - core, 3)[order]


def side_blocks_kernel(meta_ref, *refs):
    out_ref, mine_ref, right_ref = refs[-3:]
    line = mine_ref.shape[0]
    levels = [level_of(meta_ref, i, line) for i in range(line)]
    place_rows(mine_ref, (), refs[:1], levels)
    for d in (1, 2):
        for k in range(2):
            for order in (1, 2):
                is_core = taken_core(meta_ref, 0, d) == k

                @pl.when(jnp.logical_and(is_core, group_of(meta_ref, k, order) == d))
                def _():
                    place_rows(right_ref, (), [refs[2 * k + order]], levels)

        left_products(mine_ref, right_ref, out_ref, d - 1)


def corner_blocks_kernel(meta_ref, *refs):
    out_ref, mine_ref, right_ref = refs[-3:]
    line = mine_ref.shape[0]
    levels = [level_of(meta_ref, i, line) for i in range(line)]
    place_rows(mine_ref, (), refs[:1], levels)
    for k in range(2):

        @pl.when(taken_core(meta_ref, 0, 3) == k)
        def _():
            place_rows(right_ref, (), [refs[1 + k]], levels)

    left_products(mine_ref, right_ref, out_ref, 0)


def columns_kernel(slab, orders, meta_ref, *refs):
    out_ref, held_ref = refs[-2:]
    groups, _, line = held_ref.shape[:3]
    levels = [level_of(meta_ref, i, line) for i in range(line)]
    columns = pl.ds(pl.multiple_of(meta_ref[1] * slab, slab), slab)
    for k in range(2):
        for index, order in enumerate(orders):
            e = group_of(meta_ref, k, order) - orders[0]
            place_rows(held_ref, (e, k), [refs[len(orders) * k + index]], levels, columns)

    def step(i, carry):
        group, level = i // line, lax.rem(i, line)
        e, k = group // 2, lax.rem(group, 2)
        out_ref[e, k, level] = held_ref[e, k, level].T
        return carry

    lax.fori_loop(0, 2 * groups * line, step, 0)


def met_places(meta_ref, e, k):
    return [(e, k), (e, 1 - k)] + [(e ^ d, k ^ taken_core(meta_ref, e, d)) for d in (1, 2, 3)]


def side_by_side(turned_ref, places):
    line = turned_ref.shape[2]
    return jnp.concatenate(
        [turned_ref[a, b, level] for a, b in places for level in range(line)], axis=1
    )


def start_all(copies):
    for copy in copies:
        copy.start()
    return copies


def wait_all(copies):
    for copy in copies:
        copy.wait()


def shard_copies(meta_ref, refs, slots, held_ref, sems):
    copies = []
    for i, slot in enumerate(slots):
        for k in range(2):
            for order in range(4):
                source = refs[8 * slot + 4 * k + order]
                target = held_ref.at[group_of(meta_ref, k, order), k, i]
                copies.append(pltpu.make_async_copy(source, target, sems.at[len(copies)]))
    return copies


def column_copies(near_hbm, far_hbm, xt_ref, sems, used):
    parts = ((near_hbm, xt_ref.at[:3]), (far_hbm, xt_ref.at[3:]))
    return [
        pltpu.make_async_copy(source, target, sems.at[used + i])
        for i, (source, target) in enumerate(parts)
    ]


def image_parts(meta_ref, xt_ref, held_ref, levels, e, k):
    line, width, count = xt_ref.shape[2:]
    size = line * count
    slots = len(levels)
    left, right = [], []
    for d in (1, 2, 3):
        a = e ^ d
        b = k ^ taken_core(meta_ref, a, d)
        for n in range(slots):
            left.append(xt_ref[a, b, levels[n]])
            right.append(held_ref[a, b, n, :, (1 + d) * size:(2 + d) * size])
    back = matmul(jnp.concatenate(left, axis=1), jnp.concatenate(right))
    forth = row_product(
        side_by_side(xt_ref, met_places(meta_ref, e, k)),
        held_ref[e, k].reshape(slots * count, 5 * size),
    )
    return back, forth


def early_kernel(slots, meta_ref, near_hbm, far_hbm, *refs):
    acc_hbm, xt_ref, held_ref, acc_ref, sems, out_sems = refs[-6:]
    line, width, count = xt_ref.shape[2:]
    levels = [level_of(meta_ref, i, line) for i in range(slots)]
    copies = shard_copies(meta_ref, refs, range(slots), held_ref, sems)
    copies += column_copies(near_hbm, far_hbm, xt_ref, sems, len(copies))
    wait_all(start_all(copies))

    def out_copy(i):
        return pltpu.make_async_copy(
            acc_ref.at[i // 2, lax.rem(i, 2)], acc_hbm.at[i // 2, lax.rem(i, 2)], out_sems.at[i]
        )

    def step(i, carry):
        e, k = i // 2, lax.rem(i, 2)
        back, forth = image_parts(meta_ref, xt_ref, held_ref, levels, e, k)
        for level in range(line):
            acc_ref[e, k, level] = back[:, level * count:(level + 1) * count]
        for n in range(slots):
            acc_ref[e, k, levels[n]] += forth[:, n * count:(n + 1) * count]
        out_copy(i).start()
        return carry

    lax.fori_loop(0, 8, step, 0)
    for i in range(8):
        out_copy(i).wait()


def last_kernel(gain, slots, meta_ref, near_hbm, far_hbm, acc_hbm, *refs):
    out_ref, xt_ref, held_ref, acc_ref, image_ref, own_ref, cross_ref, back_ref = refs[-11:-3]
    sems, acc_sems, later_sems = refs[-3:]
    line, width, count = xt_ref.shape[2:]
    size = line * count
    slot_levels = [level_of(meta_ref, i, line) for i in range(line)]
    levels = slot_levels[line - slots:]
    copies = shard_copies(meta_ref, refs, range(line - slots, line), held_ref, sems)
    copies += column_copies(near_hbm, far_hbm, xt_ref, sems, len(copies))
    start_all(copies)

    def acc_copy(i):
        held = lax.rem(i, 2)
        return pltpu.make_async_copy(
            acc_hbm.at[i // 2, held], acc_ref.at[held], acc_sems.at[held]
        )

    for i in range(2):
        acc_copy(i).start()
    later = []
    for i in range(line):
        for k in range(2):
            for order in range(4):
                source, target = refs[8 * i + 4 * k + order], own_ref.at[k, i]
                if order:
                    e = group_of(meta_ref, k, order)
                    first = (1 + e) * size
                    first = pl.multiple_of(first, size) if order < 3 else first
                    source, target = source.at[:, pl.ds(first, size)], cross_ref.at[e - 1, k, i]
                later.append(pltpu.make_async_copy(source, target, later_sems.at[len(later)]))
    start_all(later)
    wait_all(copies)

    def step(i, carry):
        e, k = i // 2, lax.rem(i, 2)
        back, forth = image_parts(meta_ref, xt_ref, held_ref, levels, e, k)
        acc_copy(i).wait()
        for n in range(slots):
            acc_ref[k, levels[n]] += forth[:, n * count:(n + 1) * count]
        for level in range(line):
            total = acc_ref[k, level] + back[:, level * count:(level + 1) * count]
            image_ref[e, k, level] = total.astype(jnp.bfloat16)

        @pl.when(i < 6)
        def _():
            acc_copy(i + 2).start()

        return carry

    lax.fori_loop(0, 8, step, 0)
    wait_all(later)

    def finish(k, carry):
        places = [(d, k ^ taken_core(meta_ref, d, d)) for d in (1, 2, 3)]
        blocks = [cross_ref[d - 1, b].reshape(size, size) for d, b in places]
        rows = [image_ref[d, b, level] for d, b in places for level in slot_levels]
        back = matmul(jnp.concatenate(rows, axis=1), jnp.concatenate(blocks))
        for level in range(line):
            back_ref[level] = back[:, level * count:(level + 1) * count]
        forth = row_product(
            side_by_side(image_ref, met_places(meta_ref, 0, k)),
            own_ref[k].reshape(size, 5 * size),
        )
        core = meta_ref[1] ^ k
        for i, level in enumerate(slot_levels):
            second = forth[:, i * count:(i + 1) * count] + back_ref[level]
            turned = combine(xt_ref[0, k, level], image_ref[0, k, level], second, gain)
            out_ref[level, core] = turned.T
        return carry

    lax.fori_loop(0, 2, finish, 0)


def after(values, *others):
    return lax.optimization_barrier((values,) + others)[0]


def neighbour_plan(iterate, gain):
    line = lax.axis_size("col") // 2
    count, width = iterate.shape
    slab = width // (2 * line)
    size = line * count
    row_devices = lax.axis_size("row")
    place, row = lax.axis_index("col"), lax.axis_index("row")
    level, core = place // 2, place % 2
    meta = jnp.stack([level, core, row & 1, row >> 1]).astype(jnp.int32)

    def along(values, hop):
        pairs = [(2 * a + k, 2 * ((a - hop) % line) + k) for a in range(line) for k in range(2)]
        return lax.ppermute(values, "col", pairs)

    def swap(values):
        pairs = [(2 * a + k, 2 * a + 1 - k) for a in range(line) for k in range(2)]
        return lax.ppermute(values, "col", pairs)

    def across(values, turn):
        pairs = [
            (r * 2 * line + c, (r ^ (1 + (c + turn) % 2)) * 2 * line + c)
            for r in range(row_devices)
            for c in range(2 * line)
        ]
        return lax.ppermute(values, ("row", "col"), pairs)

    def sent(partial):
        return [
            along(lax.dynamic_index_in_dim(partial, (level - hop) % line, 0, False), hop)
            for hop in range(1, line)
        ]

    def summed(partial, chunks):
        total = lax.dynamic_index_in_dim(partial, level, 0, False).astype(jnp.float32)
        for chunk in chunks:
            total += chunk.astype(jnp.float32)
        return total.astype(jnp.bfloat16)

    def piece(hop):
        start = ((level - hop) % line) * (2 * slab)
        return lax.dynamic_slice(iterate, (0, start), (count, 2 * slab))

    tower = jnp.concatenate(
        [along(piece(hop), hop) if hop else piece(0) for hop in range(line)]
    )
    pair_tower = swap(tower)
    flops = 4 * size * size * slab
    held = [pltpu.VMEM((line, count, 2 * slab), jnp.bfloat16)] * 2
    own_blocks = call(
        own_blocks_kernel,
        jax.ShapeDtypeStruct((line, count, 2 * size), jnp.bfloat16),
        [meta, tower, pair_tower],
        2 * flops,
        scratch=held,
    )
    own_shard = summed(own_blocks, sent(own_blocks))
    one, two = after(across(tower, 0), own_shard), after(across(tower, 1), own_shard)
    own_ring = along(own_shard, 1)
    own_one, own_two = across(own_shard, 0), across(own_shard, 1)
    pair_one, pair_two = swap(one), swap(two)
    side_blocks = call(
        side_blocks_kernel,
        jax.ShapeDtypeStruct((line, count, 2 * size), jnp.bfloat16),
        [meta, tower, one, two, pair_one, pair_two],
        2 * flops,
        scratch=held,
    )
    def columns(orders, *blocks):
        return call(
            functools.partial(columns_kernel, slab, orders),
            jax.ShapeDtypeStruct((len(orders), 2, line, slab, count), jnp.bfloat16),
            [after(meta, own_ring)] + list(blocks),
            size * slab * 128 * len(orders),
            scratch=[pltpu.VMEM((len(orders), 2, line, count, slab), jnp.bfloat16)],
        )

    side_sent = sent(side_blocks)
    near_columns = columns((0, 1, 2), tower, one, two, pair_tower, pair_one, pair_two)
    three = after(across(one, 1), side_sent[0], side_sent[-1], near_columns)
    pair_three = swap(three)
    corner_blocks = call(
        corner_blocks_kernel,
        jax.ShapeDtypeStruct((line, count, size), jnp.bfloat16),
        [meta, tower, three, pair_three],
        flops,
        scratch=held,
    )
    far_columns = columns((3,), three, pair_three)
    side_shard = summed(side_blocks, side_sent)
    own_three = across(own_one, 1)
    corner_sent = [after(chunk, own_two, own_three) for chunk in sent(corner_blocks)]
    corner_shard = summed(corner_blocks, corner_sent)
    cross_shard = jnp.concatenate([side_shard, corner_shard], axis=1)

    cut = line // 2
    turned = (4, 2, line, slab, count)

    def wide(own, cross):
        return jnp.concatenate([own, cross], axis=1)

    cross_ring = along(cross_shard, 1)
    cross_one, cross_two = across(cross_shard, 0), across(cross_shard, 1)
    held_back = [cross_ring, cross_one, cross_two, far_columns]
    near = [wide(own_shard, cross_shard), wide(own_ring, after(cross_ring, *held_back))]
    one, two = [wide(own_one, cross_one)], [wide(own_two, cross_two)]
    three, ring = [], [near[1]]

    def pieces(slots):
        own = [[near[i], one[i], two[i], three[i]] for i in slots]
        return [v for blocks in own for v in blocks + [swap(block) for block in blocks]]

    def early():
        return call(
            functools.partial(early_kernel, cut),
            jax.ShapeDtypeStruct(turned, jnp.float32),
            [meta, near_columns, far_columns] + pieces(range(cut)),
            128 * cut * count * size * slab,
            scratch=[
                pltpu.VMEM(turned, jnp.bfloat16),
                pltpu.VMEM((4, 2, cut, count, 5 * size), jnp.bfloat16),
                pltpu.VMEM(turned, jnp.float32),
                pltpu.SemaphoreType.DMA((8 * cut + 2,)),
                pltpu.SemaphoreType.DMA((8,)),
            ],
            space=pl.ANY,
            out_space=pl.ANY,
        )

    for step in range(1, line + 1):
        done = held_back if step == 1 else [b[-1] for b in (ring, one, two, three)]
        if step == line:
            acc = early()
            done = done + [acc]
        if step == 1:
            cross_three = across(after(cross_one, *done), 1)
            three.append(wide(own_three, cross_three))
        else:
            three.append(across(after(one[-1], *done), 1))
        if step < line:
            here = after(near[step], *done)
            one.append(across(here, 0))
            two.append(across(here, 1))
        if step < line - 1:
            ring.append(along(here, 1))
            near.append(ring[-1])
    update = call(
        functools.partial(last_kernel, gain, line - cut),
        jax.ShapeDtypeStruct((line, 2, count, slab), jnp.bfloat16),
        [meta, near_columns, far_columns, acc] + pieces(range(line)),
        (128 * (line - cut) * count + 32 * size) * size * slab,
        scratch=[
            pltpu.VMEM(turned, jnp.bfloat16),
            pltpu.VMEM((4, 2, line - cut, count, 5 * size), jnp.bfloat16),
            pltpu.VMEM((2, line, slab, count), jnp.float32),
            pltpu.VMEM(turned, jnp.bfloat16),
            pltpu.VMEM((2, line, count, 5 * size), jnp.bfloat16),
            pltpu.VMEM((3, 2, line, count, size), jnp.bfloat16),
            pltpu.VMEM((line, slab, count), jnp.float32),
            pltpu.SemaphoreType.DMA((8 * (line - cut) + 2,)),
            pltpu.SemaphoreType.DMA((2,)),
            pltpu.SemaphoreType.DMA((8 * line,)),
        ],
        space=pl.ANY,
    )
    return update.reshape(2 * size, slab)


def solution(mesh):
    square_of_lines = mesh.shape["row"] == 4 and mesh.shape["col"] in (4, 6, 8)

    def program(iterate):
        gain = output_gain * math.sqrt(max(iterate.shape))
        plan = neighbour_plan if square_of_lines else gathered_plan
        return jax.shard_map(
            lambda block: plan(block, gain),
            mesh=mesh,
            in_specs=(P(("row", "col"), None),),
            out_specs=P("row", "col"),
            check_vma=False,
        )(iterate)

    return program
```

```python
import functools
import math

import jax
import jax.numpy as jnp
from jax import lax
from jax.experimental import pallas as pl
from jax.experimental.pallas import tpu as pltpu
from jax.sharding import PartitionSpec as P

linear_weight = 3.4445
cubic_weight = -4.775
quintic_weight = 2.0315
output_gain = 0.2


def gather_rows(block_rows):
    return lax.all_gather(block_rows, "row", axis=0, tiled=True)


def strided_order(panel_rows, row_devices, col_devices):
    total_rows, column_count = panel_rows.shape
    per_device = total_rows // (row_devices * col_devices)
    grouped = panel_rows.reshape(row_devices, col_devices, per_device, column_count)
    return jnp.transpose(grouped, (1, 0, 2, 3)).reshape(total_rows, column_count)


def row_product(left_rows, right_rows):
    return lax.dot_general(
        left_rows, right_rows, (((1,), (1,)), ((), ())), preferred_element_type=jnp.float32
    )


def combine(scaled_tile, image_tile, second_term, gain):
    combined = (
        linear_weight * scaled_tile.astype(jnp.float32)
        + cubic_weight * image_tile.astype(jnp.float32)
        + quintic_weight * second_term
    )
    return (gain * combined).astype(jnp.bfloat16)


def gathered_plan(iterate, gain):
    scaled_tile = lax.all_to_all(iterate, "col", split_axis=1, concat_axis=0, tiled=True)
    row_devices = lax.axis_size("row")
    col_devices = lax.axis_size("col")
    strided_rows = gather_rows(iterate)
    panel_rows = lax.all_gather(scaled_tile, "col", axis=1, tiled=True)
    gram_tile = row_product(panel_rows, strided_rows).astype(jnp.bfloat16)
    gram_wide = lax.all_gather(gram_tile, "col", axis=1, tiled=True)
    scaled_columns = strided_order(gather_rows(scaled_tile), row_devices, col_devices)
    image_tile = jnp.dot(gram_wide, scaled_columns, preferred_element_type=jnp.float32).astype(
        jnp.bfloat16
    )
    image_columns = strided_order(gather_rows(image_tile), row_devices, col_devices)
    second_term = jnp.dot(gram_wide, image_columns, preferred_element_type=jnp.float32)
    return combine(scaled_tile, image_tile, second_term, gain)


def call(
    kernel, out_shape, operands, flops, scratch=(), space=pltpu.VMEM, out_space=pltpu.VMEM
):
    specs = [pl.BlockSpec(memory_space=pltpu.SMEM)]
    specs += [pl.BlockSpec(memory_space=space)] * (len(operands) - 1)
    moved = sum(math.prod(v.shape) * v.dtype.itemsize for v in operands)
    return pl.pallas_call(
        kernel,
        in_specs=specs,
        out_specs=pl.BlockSpec(memory_space=out_space),
        out_shape=out_shape,
        scratch_shapes=list(scratch),
        compiler_params=pltpu.CompilerParams(vmem_limit_bytes=48 * 1024 * 1024),
        cost_estimate=pl.CostEstimate(flops=flops, bytes_accessed=moved, transcendentals=0),
    )(*operands)


def matmul(left, right):
    return jnp.dot(left, right, preferred_element_type=jnp.float32)


def taken_core(meta_ref, e, distance):
    return meta_ref[3] ^ (e >> 1) if distance == 2 else meta_ref[2] ^ (e & 1)


def level_of(meta_ref, slot, line):
    return lax.rem(meta_ref[0] + slot, line)


def place_rows(held_ref, lead, parts, levels, columns=slice(None)):
    half = held_ref.shape[-2] // 2
    done = 0
    for part in parts:
        for start in range(0, part.shape[0], half):
            slot, place = divmod(done + start, 2 * half)
            to = lead + (levels[slot], slice(place, place + half))
            held_ref[to] = part[start:start + half, columns]
        done += part.shape[0]


def left_products(mine_ref, right, out_ref, index):
    line, count, depth = mine_ref.shape
    size = line * count

    def step(i, carry):
        left = mine_ref[pl.ds(2 * i, 2)].reshape(2 * count, depth)
        product = row_product(left, right[...].reshape(size, depth))
        out_ref[pl.ds(2 * i, 2), :, index * size:(index + 1) * size] = product.astype(
            out_ref.dtype
        ).reshape(2, count, size)
        return carry

    lax.fori_loop(0, line // 2, step, 0)


def own_blocks_kernel(meta_ref, *refs):
    out_ref, mine_ref, pair_ref = refs[-3:]
    line = mine_ref.shape[0]
    levels = [level_of(meta_ref, i, line) for i in range(line)]
    place_rows(mine_ref, (), refs[:1], levels)
    place_rows(pair_ref, (), refs[1:2], levels)
    left_products(mine_ref, mine_ref, out_ref, 0)
    left_products(mine_ref, pair_ref, out_ref, 1)


def group_of(meta_ref, k, order):
    core = meta_ref[1] ^ k
    return (0, 1 + core, 2 - core, 3)[order]


def side_blocks_kernel(meta_ref, *refs):
    out_ref, mine_ref, right_ref = refs[-3:]
    line = mine_ref.shape[0]
    levels = [level_of(meta_ref, i, line) for i in range(line)]
    place_rows(mine_ref, (), refs[:1], levels)
    for d in (1, 2):
        for k in range(2):
            for order in (1, 2):
                is_core = taken_core(meta_ref, 0, d) == k

                @pl.when(jnp.logical_and(is_core, group_of(meta_ref, k, order) == d))
                def _():
                    place_rows(right_ref, (), [refs[2 * k + order]], levels)

        left_products(mine_ref, right_ref, out_ref, d - 1)


def corner_blocks_kernel(meta_ref, *refs):
    out_ref, mine_ref, right_ref = refs[-3:]
    line = mine_ref.shape[0]
    levels = [level_of(meta_ref, i, line) for i in range(line)]
    place_rows(mine_ref, (), refs[:1], levels)
    for k in range(2):

        @pl.when(taken_core(meta_ref, 0, 3) == k)
        def _():
            place_rows(right_ref, (), [refs[1 + k]], levels)

    left_products(mine_ref, right_ref, out_ref, 0)


def columns_kernel(slab, orders, meta_ref, *refs):
    out_ref, held_ref = refs[-2:]
    groups, _, line = held_ref.shape[:3]
    levels = [level_of(meta_ref, i, line) for i in range(line)]
    columns = pl.ds(pl.multiple_of(meta_ref[1] * slab, slab), slab)
    for k in range(2):
        for index, order in enumerate(orders):
            e = group_of(meta_ref, k, order) - orders[0]
            place_rows(held_ref, (e, k), [refs[len(orders) * k + index]], levels, columns)

    def step(i, carry):
        group, level = i // line, lax.rem(i, line)
        e, k = group // 2, lax.rem(group, 2)
        out_ref[e, k, level] = held_ref[e, k, level].T
        return carry

    lax.fori_loop(0, 2 * groups * line, step, 0)


def met_places(meta_ref, e, k):
    return [(e, k), (e, 1 - k)] + [(e ^ d, k ^ taken_core(meta_ref, e, d)) for d in (1, 2, 3)]


def side_by_side(turned_ref, places):
    line = turned_ref.shape[2]
    return jnp.concatenate(
        [turned_ref[a, b, level] for a, b in places for level in range(line)], axis=1
    )


def start_all(copies):
    for copy in copies:
        copy.start()
    return copies


def wait_all(copies):
    for copy in copies:
        copy.wait()


def shard_copies(meta_ref, refs, slots, held_ref, sems):
    copies = []
    for i, slot in enumerate(slots):
        for k in range(2):
            for order in range(4):
                source = refs[8 * slot + 4 * k + order]
                target = held_ref.at[group_of(meta_ref, k, order), k, i]
                copies.append(pltpu.make_async_copy(source, target, sems.at[len(copies)]))
    return copies


def column_copies(near_hbm, far_hbm, xt_ref, sems, used):
    parts = ((near_hbm, xt_ref.at[:3]), (far_hbm, xt_ref.at[3:]))
    return [
        pltpu.make_async_copy(source, target, sems.at[used + i])
        for i, (source, target) in enumerate(parts)
    ]


def image_parts(meta_ref, xt_ref, held_ref, levels, e, k):
    line, width, count = xt_ref.shape[2:]
    size = line * count
    slots = len(levels)
    left, right = [], []
    for d in (1, 2, 3):
        a = e ^ d
        b = k ^ taken_core(meta_ref, a, d)
        for n in range(slots):
            left.append(xt_ref[a, b, levels[n]])
            right.append(held_ref[a, b, n, :, (1 + d) * size:(2 + d) * size])
    back = matmul(jnp.concatenate(left, axis=1), jnp.concatenate(right))
    forth = row_product(
        side_by_side(xt_ref, met_places(meta_ref, e, k)),
        held_ref[e, k].reshape(slots * count, 5 * size),
    )
    return back, forth


def early_kernel(slots, meta_ref, near_hbm, far_hbm, *refs):
    acc_hbm, xt_ref, held_ref, acc_ref, sems, out_sems = refs[-6:]
    line, width, count = xt_ref.shape[2:]
    levels = [level_of(meta_ref, i, line) for i in range(slots)]
    copies = shard_copies(meta_ref, refs, range(slots), held_ref, sems)
    copies += column_copies(near_hbm, far_hbm, xt_ref, sems, len(copies))
    wait_all(start_all(copies))

    def out_copy(i):
        return pltpu.make_async_copy(
            acc_ref.at[i // 2, lax.rem(i, 2)], acc_hbm.at[i // 2, lax.rem(i, 2)], out_sems.at[i]
        )

    def step(i, carry):
        e, k = i // 2, lax.rem(i, 2)
        back, forth = image_parts(meta_ref, xt_ref, held_ref, levels, e, k)
        for level in range(line):
            acc_ref[e, k, level] = back[:, level * count:(level + 1) * count]
        for n in range(slots):
            acc_ref[e, k, levels[n]] += forth[:, n * count:(n + 1) * count]
        out_copy(i).start()
        return carry

    lax.fori_loop(0, 8, step, 0)
    for i in range(8):
        out_copy(i).wait()


def last_kernel(gain, slots, meta_ref, near_hbm, far_hbm, acc_hbm, *refs):
    out_ref, xt_ref, held_ref, acc_ref, image_ref, own_ref, cross_ref, back_ref = refs[-11:-3]
    sems, acc_sems, later_sems = refs[-3:]
    line, width, count = xt_ref.shape[2:]
    size = line * count
    slot_levels = [level_of(meta_ref, i, line) for i in range(line)]
    levels = slot_levels[line - slots:]
    copies = shard_copies(meta_ref, refs, range(line - slots, line), held_ref, sems)
    copies += column_copies(near_hbm, far_hbm, xt_ref, sems, len(copies))
    start_all(copies)

    def acc_copy(i):
        held = lax.rem(i, 2)
        return pltpu.make_async_copy(
            acc_hbm.at[i // 2, held], acc_ref.at[held], acc_sems.at[held]
        )

    for i in range(2):
        acc_copy(i).start()
    later = []
    for i in range(line):
        for k in range(2):
            for order in range(4):
                source, target = refs[8 * i + 4 * k + order], own_ref.at[k, i]
                if order:
                    e = group_of(meta_ref, k, order)
                    first = (1 + e) * size
                    first = pl.multiple_of(first, size) if order < 3 else first
                    source, target = source.at[:, pl.ds(first, size)], cross_ref.at[e - 1, k, i]
                later.append(pltpu.make_async_copy(source, target, later_sems.at[len(later)]))
    start_all(later)
    wait_all(copies)

    def step(i, carry):
        e, k = i // 2, lax.rem(i, 2)
        back, forth = image_parts(meta_ref, xt_ref, held_ref, levels, e, k)
        acc_copy(i).wait()
        for n in range(slots):
            acc_ref[k, levels[n]] += forth[:, n * count:(n + 1) * count]
        for level in range(line):
            total = acc_ref[k, level] + back[:, level * count:(level + 1) * count]
            image_ref[e, k, level] = total.astype(jnp.bfloat16)

        @pl.when(i < 6)
        def _():
            acc_copy(i + 2).start()

        return carry

    lax.fori_loop(0, 8, step, 0)
    wait_all(later)

    def finish(k, carry):
        places = [(d, k ^ taken_core(meta_ref, d, d)) for d in (1, 2, 3)]
        blocks = [cross_ref[d - 1, b].reshape(size, size) for d, b in places]
        rows = [image_ref[d, b, level] for d, b in places for level in slot_levels]
        back = matmul(jnp.concatenate(rows, axis=1), jnp.concatenate(blocks))
        for level in range(line):
            back_ref[level] = back[:, level * count:(level + 1) * count]
        forth = row_product(
            side_by_side(image_ref, met_places(meta_ref, 0, k)),
            own_ref[k].reshape(size, 5 * size),
        )
        core = meta_ref[1] ^ k
        for i, level in enumerate(slot_levels):
            second = forth[:, i * count:(i + 1) * count] + back_ref[level]
            turned = combine(xt_ref[0, k, level], image_ref[0, k, level], second, gain)
            out_ref[level, core] = turned.T
        return carry

    lax.fori_loop(0, 2, finish, 0)


def after(values, *others):
    return lax.optimization_barrier((values,) + others)[0]


def neighbour_plan(iterate, gain):
    line = lax.axis_size("col") // 2
    count, width = iterate.shape
    slab = width // (2 * line)
    size = line * count
    row_devices = lax.axis_size("row")
    place, row = lax.axis_index("col"), lax.axis_index("row")
    level, core = place // 2, place % 2
    meta = jnp.stack([level, core, row & 1, row >> 1]).astype(jnp.int32)

    def along(values, hop):
        pairs = [(2 * a + k, 2 * ((a - hop) % line) + k) for a in range(line) for k in range(2)]
        return lax.ppermute(values, "col", pairs)

    def swap(values):
        pairs = [(2 * a + k, 2 * a + 1 - k) for a in range(line) for k in range(2)]
        return lax.ppermute(values, "col", pairs)

    def across(values, turn):
        pairs = [
            (r * 2 * line + c, (r ^ (1 + (c + turn) % 2)) * 2 * line + c)
            for r in range(row_devices)
            for c in range(2 * line)
        ]
        return lax.ppermute(values, ("row", "col"), pairs)

    def sent(partial):
        return [
            along(lax.dynamic_index_in_dim(partial, (level - hop) % line, 0, False), hop)
            for hop in range(1, line)
        ]

    def summed(partial, chunks):
        total = lax.dynamic_index_in_dim(partial, level, 0, False).astype(jnp.float32)
        for chunk in chunks:
            total += chunk.astype(jnp.float32)
        return total.astype(jnp.bfloat16)

    def piece(hop):
        start = ((level - hop) % line) * (2 * slab)
        return lax.dynamic_slice(iterate, (0, start), (count, 2 * slab))

    tower = jnp.concatenate(
        [along(piece(hop), hop) if hop else piece(0) for hop in range(line)]
    )
    pair_tower = swap(tower)
    flops = 4 * size * size * slab
    held = [pltpu.VMEM((line, count, 2 * slab), jnp.bfloat16)] * 2
    own_blocks = call(
        own_blocks_kernel,
        jax.ShapeDtypeStruct((line, count, 2 * size), jnp.bfloat16),
        [meta, tower, pair_tower],
        2 * flops,
        scratch=held,
    )
    own_shard = summed(own_blocks, sent(own_blocks))
    one, two = after(across(tower, 0), own_shard), after(across(tower, 1), own_shard)
    own_ring = along(own_shard, 1)
    own_one, own_two = across(own_shard, 0), across(own_shard, 1)
    pair_one, pair_two = swap(one), swap(two)
    side_blocks = call(
        side_blocks_kernel,
        jax.ShapeDtypeStruct((line, count, 2 * size), jnp.bfloat16),
        [meta, tower, one, two, pair_one, pair_two],
        2 * flops,
        scratch=held,
    )
    def columns(orders, *blocks):
        return call(
            functools.partial(columns_kernel, slab, orders),
            jax.ShapeDtypeStruct((len(orders), 2, line, slab, count), jnp.bfloat16),
            [after(meta, own_ring)] + list(blocks),
            size * slab * 128 * len(orders),
            scratch=[pltpu.VMEM((len(orders), 2, line, count, slab), jnp.bfloat16)],
        )

    side_sent = sent(side_blocks)
    near_columns = columns((0, 1, 2), tower, one, two, pair_tower, pair_one, pair_two)
    three = after(across(one, 1), side_sent[0], side_sent[-1], near_columns)
    pair_three = swap(three)
    corner_blocks = call(
        corner_blocks_kernel,
        jax.ShapeDtypeStruct((line, count, size), jnp.bfloat16),
        [meta, tower, three, pair_three],
        flops,
        scratch=held,
    )
    far_columns = columns((3,), three, pair_three)
    side_shard = summed(side_blocks, side_sent)
    own_three = across(own_one, 1)
    corner_sent = [after(chunk, own_two, own_three, far_columns) for chunk in sent(corner_blocks)]
    corner_shard = summed(corner_blocks, corner_sent)
    cross_shard = jnp.concatenate([side_shard, corner_shard], axis=1)

    cut = line // 2
    turned = (4, 2, line, slab, count)

    def wide(own, cross):
        return jnp.concatenate([own, cross], axis=1)

    cross_ring = along(cross_shard, 1)
    cross_one, cross_two = across(cross_shard, 0), across(cross_shard, 1)
    held_back = [cross_ring, cross_one, cross_two]
    near = [wide(own_shard, cross_shard), wide(own_ring, after(cross_ring, *held_back))]
    one, two = [wide(own_one, cross_one)], [wide(own_two, cross_two)]
    three, ring = [], [near[1]]

    def pieces(slots):
        own = [[near[i], one[i], two[i], three[i]] for i in slots]
        return [v for blocks in own for v in blocks + [swap(block) for block in blocks]]

    def early():
        return call(
            functools.partial(early_kernel, cut),
            jax.ShapeDtypeStruct(turned, jnp.float32),
            [meta, near_columns, far_columns] + pieces(range(cut)),
            128 * cut * count * size * slab,
            scratch=[
                pltpu.VMEM(turned, jnp.bfloat16),
                pltpu.VMEM((4, 2, cut, count, 5 * size), jnp.bfloat16),
                pltpu.VMEM(turned, jnp.float32),
                pltpu.SemaphoreType.DMA((8 * cut + 2,)),
                pltpu.SemaphoreType.DMA((8,)),
            ],
            space=pl.ANY,
            out_space=pl.ANY,
        )

    late = line - 2 if line > 3 else line
    for step in range(1, line + 1):
        done = held_back if step == 1 else [b[-1] for b in (ring, one, two, three)]
        if step == line:
            acc = early()
            done = done + [two[-2], acc]
        if step == 1:
            cross_three = across(after(cross_one, *done), 1)
            three.append(wide(own_three, cross_three))
        elif step == late + 1:
            two.append(across(after(near[late], *done), 1))
            three.append(along(after(three[-1], *done), 1))
        else:
            three.append(across(after(one[-1], *done), 1))
        if step < line:
            here = after(near[step], *done)
            one.append(across(here, 0))
            if step != late:
                two.append(across(here, 1))
        if step < line - 1:
            ring.append(along(here, 1))
            near.append(ring[-1])
    update = call(
        functools.partial(last_kernel, gain, line - cut),
        jax.ShapeDtypeStruct((line, 2, count, slab), jnp.bfloat16),
        [meta, near_columns, far_columns, acc] + pieces(range(line)),
        (128 * (line - cut) * count + 32 * size) * size * slab,
        scratch=[
            pltpu.VMEM(turned, jnp.bfloat16),
            pltpu.VMEM((4, 2, line - cut, count, 5 * size), jnp.bfloat16),
            pltpu.VMEM((2, line, slab, count), jnp.float32),
            pltpu.VMEM(turned, jnp.bfloat16),
            pltpu.VMEM((2, line, count, 5 * size), jnp.bfloat16),
            pltpu.VMEM((3, 2, line, count, size), jnp.bfloat16),
            pltpu.VMEM((line, slab, count), jnp.float32),
            pltpu.SemaphoreType.DMA((8 * (line - cut) + 2,)),
            pltpu.SemaphoreType.DMA((2,)),
            pltpu.SemaphoreType.DMA((8 * line,)),
        ],
        space=pl.ANY,
    )
    return update.reshape(2 * size, slab)


def solution(mesh):
    square_of_lines = mesh.shape["row"] == 4 and mesh.shape["col"] in (4, 6, 8)

    def program(iterate):
        gain = output_gain * math.sqrt(max(iterate.shape))
        plan = neighbour_plan if square_of_lines else gathered_plan
        return jax.shard_map(
            lambda block: plan(block, gain),
            mesh=mesh,
            in_specs=(P(("row", "col"), None),),
            out_specs=P("row", "col"),
            check_vma=False,
        )(iterate)

    return program
```

```python
import functools
import math

import jax
import jax.numpy as jnp
from jax import lax
from jax.experimental import pallas as pl
from jax.experimental.pallas import tpu as pltpu
from jax.sharding import PartitionSpec as P

linear_weight = 3.4445
cubic_weight = -4.775
quintic_weight = 2.0315
output_gain = 0.2


def gather_rows(block_rows):
    return lax.all_gather(block_rows, "row", axis=0, tiled=True)


def strided_order(panel_rows, row_devices, col_devices):
    total_rows, column_count = panel_rows.shape
    per_device = total_rows // (row_devices * col_devices)
    grouped = panel_rows.reshape(row_devices, col_devices, per_device, column_count)
    return jnp.transpose(grouped, (1, 0, 2, 3)).reshape(total_rows, column_count)


def row_product(left_rows, right_rows):
    return lax.dot_general(
        left_rows, right_rows, (((1,), (1,)), ((), ())), preferred_element_type=jnp.float32
    )


def combine(scaled_tile, image_tile, second_term, gain):
    combined = (
        linear_weight * scaled_tile.astype(jnp.float32)
        + cubic_weight * image_tile.astype(jnp.float32)
        + quintic_weight * second_term
    )
    return (gain * combined).astype(jnp.bfloat16)


def gathered_plan(iterate, gain):
    scaled_tile = lax.all_to_all(iterate, "col", split_axis=1, concat_axis=0, tiled=True)
    row_devices = lax.axis_size("row")
    col_devices = lax.axis_size("col")
    strided_rows = gather_rows(iterate)
    panel_rows = lax.all_gather(scaled_tile, "col", axis=1, tiled=True)
    gram_tile = row_product(panel_rows, strided_rows).astype(jnp.bfloat16)
    gram_wide = lax.all_gather(gram_tile, "col", axis=1, tiled=True)
    scaled_columns = strided_order(gather_rows(scaled_tile), row_devices, col_devices)
    image_tile = jnp.dot(gram_wide, scaled_columns, preferred_element_type=jnp.float32).astype(
        jnp.bfloat16
    )
    image_columns = strided_order(gather_rows(image_tile), row_devices, col_devices)
    second_term = jnp.dot(gram_wide, image_columns, preferred_element_type=jnp.float32)
    return combine(scaled_tile, image_tile, second_term, gain)


def call(
    kernel, out_shape, operands, flops, scratch=(), space=pltpu.VMEM, out_space=pltpu.VMEM
):
    specs = [pl.BlockSpec(memory_space=pltpu.SMEM)]
    specs += [pl.BlockSpec(memory_space=space)] * (len(operands) - 1)
    moved = sum(math.prod(v.shape) * v.dtype.itemsize for v in operands)
    return pl.pallas_call(
        kernel,
        in_specs=specs,
        out_specs=pl.BlockSpec(memory_space=out_space),
        out_shape=out_shape,
        scratch_shapes=list(scratch),
        compiler_params=pltpu.CompilerParams(vmem_limit_bytes=48 * 1024 * 1024),
        cost_estimate=pl.CostEstimate(flops=flops, bytes_accessed=moved, transcendentals=0),
    )(*operands)


def matmul(left, right):
    return jnp.dot(left, right, preferred_element_type=jnp.float32)


def taken_core(meta_ref, e, distance):
    return meta_ref[3] ^ (e >> 1) if distance == 2 else meta_ref[2] ^ (e & 1)


def level_of(meta_ref, slot, line):
    return lax.rem(meta_ref[0] + slot, line)


def place_rows(held_ref, lead, parts, levels, columns=slice(None)):
    half = held_ref.shape[-2] // 2
    done = 0
    for part in parts:
        for start in range(0, part.shape[0], half):
            slot, place = divmod(done + start, 2 * half)
            to = lead + (levels[slot], slice(place, place + half))
            held_ref[to] = part[start:start + half, columns]
        done += part.shape[0]


def left_products(mine_ref, right, out_ref, index):
    line, count, depth = mine_ref.shape
    size = line * count
    product = row_product(
        mine_ref[...].reshape(size, depth), right[...].reshape(size, depth)
    )
    out_ref[:, :, index * size:(index + 1) * size] = product.astype(out_ref.dtype).reshape(
        line, count, size
    )


def own_blocks_kernel(meta_ref, *refs):
    out_ref, mine_ref, pair_ref = refs[-3:]
    line = mine_ref.shape[0]
    levels = [level_of(meta_ref, i, line) for i in range(line)]
    place_rows(mine_ref, (), refs[:1], levels)
    place_rows(pair_ref, (), refs[1:2], levels)
    left_products(mine_ref, mine_ref, out_ref, 0)
    left_products(mine_ref, pair_ref, out_ref, 1)


def group_of(meta_ref, k, order):
    core = meta_ref[1] ^ k
    return (0, 1 + core, 2 - core, 3)[order]


def side_blocks_kernel(meta_ref, *refs):
    out_ref, mine_ref, right_ref = refs[-3:]
    line = mine_ref.shape[0]
    levels = [level_of(meta_ref, i, line) for i in range(line)]
    place_rows(mine_ref, (), refs[:1], levels)
    for d in (1, 2):
        for k in range(2):
            for order in (1, 2):
                is_core = taken_core(meta_ref, 0, d) == k

                @pl.when(jnp.logical_and(is_core, group_of(meta_ref, k, order) == d))
                def _():
                    place_rows(right_ref, (), [refs[2 * k + order]], levels)

        left_products(mine_ref, right_ref, out_ref, d - 1)


def corner_blocks_kernel(meta_ref, *refs):
    out_ref, mine_ref, right_ref = refs[-3:]
    line = mine_ref.shape[0]
    levels = [level_of(meta_ref, i, line) for i in range(line)]
    place_rows(mine_ref, (), refs[:1], levels)
    for k in range(2):

        @pl.when(taken_core(meta_ref, 0, 3) == k)
        def _():
            place_rows(right_ref, (), [refs[1 + k]], levels)

    left_products(mine_ref, right_ref, out_ref, 0)


def columns_kernel(slab, orders, meta_ref, *refs):
    out_ref, held_ref = refs[-2:]
    groups, _, line = held_ref.shape[:3]
    levels = [level_of(meta_ref, i, line) for i in range(line)]
    columns = pl.ds(pl.multiple_of(meta_ref[1] * slab, slab), slab)
    for k in range(2):
        for index, order in enumerate(orders):
            e = group_of(meta_ref, k, order) - orders[0]
            place_rows(held_ref, (e, k), [refs[len(orders) * k + index]], levels, columns)

    def step(i, carry):
        group, level = i // line, lax.rem(i, line)
        e, k = group // 2, lax.rem(group, 2)
        out_ref[e, k, level] = held_ref[e, k, level].T
        return carry

    lax.fori_loop(0, 2 * groups * line, step, 0)


def met_places(meta_ref, e, k):
    return [(e, k), (e, 1 - k)] + [(e ^ d, k ^ taken_core(meta_ref, e, d)) for d in (1, 2, 3)]


def side_by_side(turned_ref, places):
    line = turned_ref.shape[2]
    return jnp.concatenate(
        [turned_ref[a, b, level] for a, b in places for level in range(line)], axis=1
    )


def start_all(copies):
    for copy in copies:
        copy.start()
    return copies


def wait_all(copies):
    for copy in copies:
        copy.wait()


def shard_copies(meta_ref, refs, slots, held_ref, sems):
    copies = []
    for i, slot in enumerate(slots):
        for k in range(2):
            for order in range(4):
                source = refs[8 * slot + 4 * k + order]
                target = held_ref.at[group_of(meta_ref, k, order), k, i]
                copies.append(pltpu.make_async_copy(source, target, sems.at[len(copies)]))
    return copies


def column_copies(near_hbm, far_hbm, xt_ref, sems, used):
    parts = ((near_hbm, xt_ref.at[:3]), (far_hbm, xt_ref.at[3:]))
    return [
        pltpu.make_async_copy(source, target, sems.at[used + i])
        for i, (source, target) in enumerate(parts)
    ]


def by_columns(meta_ref, xt_ref, held_ref, levels, e, k):
    line, width, count = xt_ref.shape[2:]
    size = line * count
    left, right = [], []
    for d in (1, 2, 3):
        a = e ^ d
        b = k ^ taken_core(meta_ref, a, d)
        for n, level in enumerate(levels):
            left.append(xt_ref[a, b, level])
            right.append(held_ref[a, b, n, :, (1 + d) * size:(2 + d) * size])
    return matmul(jnp.concatenate(left, axis=1), jnp.concatenate(right))


def by_rows(meta_ref, xt_ref, held_ref, e, k):
    slots, count, width = held_ref.shape[2:]
    return row_product(
        side_by_side(xt_ref, met_places(meta_ref, e, k)),
        held_ref[e, k].reshape(slots * count, width),
    )


def when_held(copies, xt_copies, slots, body):
    wait_all(xt_copies)
    for e in range(4):
        if e == 1:
            wait_all([copies[8 * i + 4 * k + o] for i in range(slots) for k in (0, 1) for o in (1, 2)])
        if e in (0, 3):
            wait_all([copies[8 * i + 4 * k + e] for i in range(slots) for k in (0, 1)])

        def step(k, carry, e=e):
            body(e, k)
            return carry

        lax.fori_loop(0, 2, step, 0)


def image_parts(meta_ref, xt_ref, held_ref, levels, e, k):
    back = by_columns(meta_ref, xt_ref, held_ref, levels, e, k)
    return back, by_rows(meta_ref, xt_ref, held_ref, e, k)


def early_kernel(slots, meta_ref, near_hbm, far_hbm, *refs):
    acc_hbm, xt_ref, held_ref, acc_ref, sems, out_sems = refs[-6:]
    line, width, count = xt_ref.shape[2:]
    levels = [level_of(meta_ref, i, line) for i in range(slots)]
    copies = shard_copies(meta_ref, refs, range(slots), held_ref, sems)
    xt_copies = start_all(column_copies(near_hbm, far_hbm, xt_ref, sems, len(copies)))
    start_all(copies)
    other_levels = [level_of(meta_ref, i, line) for i in range(slots, line)]

    def rows_first(e, k):
        forth = by_rows(meta_ref, xt_ref, held_ref, e, k)
        for n, level in enumerate(levels):
            acc_ref[e, k, level] = forth[:, n * count:(n + 1) * count]
        for level in other_levels:
            acc_ref[e, k, level] = jnp.zeros((width, count), acc_ref.dtype)

    when_held(copies, xt_copies, slots, rows_first)

    def out_copy(i):
        return pltpu.make_async_copy(
            acc_ref.at[i // 2, lax.rem(i, 2)], acc_hbm.at[i // 2, lax.rem(i, 2)], out_sems.at[i]
        )

    def step(i, carry):
        e, k = i // 2, lax.rem(i, 2)
        back = by_columns(meta_ref, xt_ref, held_ref, levels, e, k)
        for level in range(line):
            acc_ref[e, k, level] += back[:, level * count:(level + 1) * count]
        out_copy(i).start()
        return carry

    lax.fori_loop(0, 8, step, 0)
    for i in range(8):
        out_copy(i).wait()


def last_kernel(gain, slots, meta_ref, near_hbm, far_hbm, acc_hbm, *refs):
    out_ref, xt_ref, held_ref, acc_ref, image_ref, own_ref, cross_ref, back_ref = refs[-11:-3]
    sems, acc_sems, later_sems = refs[-3:]
    line, width, count = xt_ref.shape[2:]
    size = line * count
    slot_levels = [level_of(meta_ref, i, line) for i in range(line)]
    levels = slot_levels[line - slots:]
    copies = shard_copies(meta_ref, refs, range(line - slots, line), held_ref, sems)
    copies += column_copies(near_hbm, far_hbm, xt_ref, sems, len(copies))
    start_all(copies)

    def acc_copy(i):
        held = lax.rem(i, 2)
        return pltpu.make_async_copy(
            acc_hbm.at[i // 2, held], acc_ref.at[held], acc_sems.at[held]
        )

    for i in range(2):
        acc_copy(i).start()
    later = []
    for i in range(line):
        for k in range(2):
            for order in range(4):
                source, target = refs[8 * i + 4 * k + order], own_ref.at[k, i]
                if order:
                    e = group_of(meta_ref, k, order)
                    first = (1 + e) * size
                    first = pl.multiple_of(first, size) if order < 3 else first
                    source, target = source.at[:, pl.ds(first, size)], cross_ref.at[e - 1, k, i]
                later.append(pltpu.make_async_copy(source, target, later_sems.at[len(later)]))
    start_all(later)
    wait_all(copies)

    def step(i, carry):
        e, k = i // 2, lax.rem(i, 2)
        back, forth = image_parts(meta_ref, xt_ref, held_ref, levels, e, k)
        acc_copy(i).wait()
        for n in range(slots):
            acc_ref[k, levels[n]] += forth[:, n * count:(n + 1) * count]
        for level in range(line):
            total = acc_ref[k, level] + back[:, level * count:(level + 1) * count]
            image_ref[e, k, level] = total.astype(jnp.bfloat16)

        @pl.when(i < 6)
        def _():
            acc_copy(i + 2).start()

        return carry

    lax.fori_loop(0, 8, step, 0)
    wait_all(later)

    def finish(k, carry):
        places = [(d, k ^ taken_core(meta_ref, d, d)) for d in (1, 2, 3)]
        blocks = [cross_ref[d - 1, b].reshape(size, size) for d, b in places]
        rows = [image_ref[d, b, level] for d, b in places for level in slot_levels]
        back = matmul(jnp.concatenate(rows, axis=1), jnp.concatenate(blocks))
        for level in range(line):
            back_ref[level] = back[:, level * count:(level + 1) * count]
        forth = row_product(
            side_by_side(image_ref, met_places(meta_ref, 0, k)),
            own_ref[k].reshape(size, 5 * size),
        )
        core = meta_ref[1] ^ k
        for i, level in enumerate(slot_levels):
            second = forth[:, i * count:(i + 1) * count] + back_ref[level]
            turned = combine(xt_ref[0, k, level], image_ref[0, k, level], second, gain)
            out_ref[level, core] = turned.T
        return carry

    lax.fori_loop(0, 2, finish, 0)


def after(values, *others):
    return lax.optimization_barrier((values,) + others)[0]


def neighbour_plan(iterate, gain):
    line = lax.axis_size("col") // 2
    count, width = iterate.shape
    slab = width // (2 * line)
    size = line * count
    row_devices = lax.axis_size("row")
    place, row = lax.axis_index("col"), lax.axis_index("row")
    level, core = place // 2, place % 2
    meta = jnp.stack([level, core, row & 1, row >> 1]).astype(jnp.int32)

    def along(values, hop):
        pairs = [(2 * a + k, 2 * ((a - hop) % line) + k) for a in range(line) for k in range(2)]
        return lax.ppermute(values, "col", pairs)

    def swap(values):
        pairs = [(2 * a + k, 2 * a + 1 - k) for a in range(line) for k in range(2)]
        return lax.ppermute(values, "col", pairs)

    def across(values, turn):
        pairs = [
            (r * 2 * line + c, (r ^ (1 + (c + turn) % 2)) * 2 * line + c)
            for r in range(row_devices)
            for c in range(2 * line)
        ]
        return lax.ppermute(values, ("row", "col"), pairs)

    def sent(partial):
        return [
            along(lax.dynamic_index_in_dim(partial, (level - hop) % line, 0, False), hop)
            for hop in range(1, line)
        ]

    def summed(partial, chunks):
        total = lax.dynamic_index_in_dim(partial, level, 0, False).astype(jnp.float32)
        for chunk in chunks:
            total += chunk.astype(jnp.float32)
        return total.astype(jnp.bfloat16)

    def piece(hop):
        start = ((level - hop) % line) * (2 * slab)
        return lax.dynamic_slice(iterate, (0, start), (count, 2 * slab))

    tower = jnp.concatenate(
        [along(piece(hop), hop) if hop else piece(0) for hop in range(line)]
    )
    pair_tower = swap(tower)
    flops = 4 * size * size * slab
    held = [pltpu.VMEM((line, count, 2 * slab), jnp.bfloat16)] * 2
    own_blocks = call(
        own_blocks_kernel,
        jax.ShapeDtypeStruct((line, count, 2 * size), jnp.bfloat16),
        [meta, tower, pair_tower],
        2 * flops,
        scratch=held,
    )
    own_shard = summed(own_blocks, sent(own_blocks))
    one, two = after(across(tower, 0), own_shard), after(across(tower, 1), own_shard)
    own_ring = along(own_shard, 1)
    own_one, own_two = across(own_shard, 0), across(own_shard, 1)
    pair_one, pair_two = swap(one), swap(two)
    side_blocks = call(
        side_blocks_kernel,
        jax.ShapeDtypeStruct((line, count, 2 * size), jnp.bfloat16),
        [meta, tower, one, two, pair_one, pair_two],
        2 * flops,
        scratch=held,
    )
    def columns(orders, *blocks):
        return call(
            functools.partial(columns_kernel, slab, orders),
            jax.ShapeDtypeStruct((len(orders), 2, line, slab, count), jnp.bfloat16),
            [after(meta, own_ring)] + list(blocks),
            size * slab * 128 * len(orders),
            scratch=[pltpu.VMEM((len(orders), 2, line, count, slab), jnp.bfloat16)],
        )

    side_sent = sent(side_blocks)
    near_columns = columns((0, 1, 2), tower, one, two, pair_tower, pair_one, pair_two)
    three = after(across(one, 1), side_sent[0], side_sent[-1], near_columns)
    pair_three = swap(three)
    corner_blocks = call(
        corner_blocks_kernel,
        jax.ShapeDtypeStruct((line, count, size), jnp.bfloat16),
        [meta, tower, three, pair_three],
        flops,
        scratch=held,
    )
    far_columns = columns((3,), three, pair_three)
    side_shard = summed(side_blocks, side_sent)
    own_three = across(own_one, 1)
    corner_sent = [after(chunk, own_two, own_three, far_columns) for chunk in sent(corner_blocks)]
    corner_shard = summed(corner_blocks, corner_sent)
    cross_shard = jnp.concatenate([side_shard, corner_shard], axis=1)

    cut = line // 2
    turned = (4, 2, line, slab, count)

    def wide(own, cross):
        return jnp.concatenate([own, cross], axis=1)

    cross_ring = along(cross_shard, 1)
    cross_one, cross_two = across(cross_shard, 0), across(cross_shard, 1)
    held_back = [cross_ring, cross_one, cross_two]
    near = [wide(own_shard, cross_shard), wide(own_ring, after(cross_ring, *held_back))]
    one, two = [wide(own_one, cross_one)], [wide(own_two, cross_two)]
    three, ring = [], [near[1]]

    def pieces(slots):
        own = [[near[i], one[i], two[i], three[i]] for i in slots]
        return [v for blocks in own for v in blocks + [swap(block) for block in blocks]]

    def early():
        return call(
            functools.partial(early_kernel, cut),
            jax.ShapeDtypeStruct(turned, jnp.float32),
            [meta, near_columns, far_columns] + pieces(range(cut)),
            128 * cut * count * size * slab,
            scratch=[
                pltpu.VMEM(turned, jnp.bfloat16),
                pltpu.VMEM((4, 2, cut, count, 5 * size), jnp.bfloat16),
                pltpu.VMEM(turned, jnp.float32),
                pltpu.SemaphoreType.DMA((8 * cut + 2,)),
                pltpu.SemaphoreType.DMA((8,)),
            ],
            space=pl.ANY,
            out_space=pl.ANY,
        )

    late = line - 2 if line > 3 else line
    for step in range(1, line + 1):
        done = held_back if step == 1 else [b[-1] for b in (ring, one, two, three)]
        if step == line:
            acc = early()
            done = done + [two[-2], acc]
        if step == 1:
            cross_three = across(after(cross_one, *done), 1)
            three.append(wide(own_three, cross_three))
        elif step == late + 1:
            two.append(across(after(near[late], *done), 1))
            three.append(along(after(three[-1], *done), 1))
        else:
            three.append(across(after(one[-1], *done), 1))
        if step < line:
            here = after(near[step], *done)
            one.append(across(here, 0))
            if step != late:
                two.append(across(here, 1))
        if step < line - 1:
            ring.append(along(here, 1))
            near.append(ring[-1])
    update = call(
        functools.partial(last_kernel, gain, line - cut),
        jax.ShapeDtypeStruct((line, 2, count, slab), jnp.bfloat16),
        [meta, near_columns, far_columns, acc] + pieces(range(line)),
        (128 * (line - cut) * count + 32 * size) * size * slab,
        scratch=[
            pltpu.VMEM(turned, jnp.bfloat16),
            pltpu.VMEM((4, 2, line - cut, count, 5 * size), jnp.bfloat16),
            pltpu.VMEM((2, line, slab, count), jnp.float32),
            pltpu.VMEM(turned, jnp.bfloat16),
            pltpu.VMEM((2, line, count, 5 * size), jnp.bfloat16),
            pltpu.VMEM((3, 2, line, count, size), jnp.bfloat16),
            pltpu.VMEM((line, slab, count), jnp.float32),
            pltpu.SemaphoreType.DMA((8 * (line - cut) + 2,)),
            pltpu.SemaphoreType.DMA((2,)),
            pltpu.SemaphoreType.DMA((8 * line,)),
        ],
        space=pl.ANY,
    )
    return update.reshape(2 * size, slab)


def solution(mesh):
    square_of_lines = mesh.shape["row"] == 4 and mesh.shape["col"] in (4, 6, 8)

    def program(iterate):
        gain = output_gain * math.sqrt(max(iterate.shape))
        plan = neighbour_plan if square_of_lines else gathered_plan
        return jax.shard_map(
            lambda block: plan(block, gain),
            mesh=mesh,
            in_specs=(P(("row", "col"), None),),
            out_specs=P("row", "col"),
            check_vma=False,
        )(iterate)

    return program
```

```python
import functools
import math

import jax
import jax.numpy as jnp
from jax import lax
from jax.experimental import pallas as pl
from jax.experimental.pallas import tpu as pltpu
from jax.sharding import PartitionSpec as P

linear_weight = 3.4445
cubic_weight = -4.775
quintic_weight = 2.0315
output_gain = 0.2


def gather_rows(block_rows):
    return lax.all_gather(block_rows, "row", axis=0, tiled=True)


def strided_order(panel_rows, row_devices, col_devices):
    total_rows, column_count = panel_rows.shape
    per_device = total_rows // (row_devices * col_devices)
    grouped = panel_rows.reshape(row_devices, col_devices, per_device, column_count)
    return jnp.transpose(grouped, (1, 0, 2, 3)).reshape(total_rows, column_count)


def row_product(left_rows, right_rows):
    return lax.dot_general(
        left_rows, right_rows, (((1,), (1,)), ((), ())), preferred_element_type=jnp.float32
    )


def combine(scaled_tile, image_tile, second_term, gain):
    combined = (
        linear_weight * scaled_tile.astype(jnp.float32)
        + cubic_weight * image_tile.astype(jnp.float32)
        + quintic_weight * second_term
    )
    return (gain * combined).astype(jnp.bfloat16)


def gathered_plan(iterate, gain):
    scaled_tile = lax.all_to_all(iterate, "col", split_axis=1, concat_axis=0, tiled=True)
    row_devices = lax.axis_size("row")
    col_devices = lax.axis_size("col")
    strided_rows = gather_rows(iterate)
    panel_rows = lax.all_gather(scaled_tile, "col", axis=1, tiled=True)
    gram_tile = row_product(panel_rows, strided_rows).astype(jnp.bfloat16)
    gram_wide = lax.all_gather(gram_tile, "col", axis=1, tiled=True)
    scaled_columns = strided_order(gather_rows(scaled_tile), row_devices, col_devices)
    image_tile = jnp.dot(gram_wide, scaled_columns, preferred_element_type=jnp.float32).astype(
        jnp.bfloat16
    )
    image_columns = strided_order(gather_rows(image_tile), row_devices, col_devices)
    second_term = jnp.dot(gram_wide, image_columns, preferred_element_type=jnp.float32)
    return combine(scaled_tile, image_tile, second_term, gain)


def call(
    kernel, out_shape, operands, flops, scratch=(), space=pltpu.VMEM, out_space=pltpu.VMEM
):
    specs = [pl.BlockSpec(memory_space=pltpu.SMEM)]
    specs += [pl.BlockSpec(memory_space=space)] * (len(operands) - 1)
    moved = sum(math.prod(v.shape) * v.dtype.itemsize for v in operands)
    return pl.pallas_call(
        kernel,
        in_specs=specs,
        out_specs=pl.BlockSpec(memory_space=out_space),
        out_shape=out_shape,
        scratch_shapes=list(scratch),
        compiler_params=pltpu.CompilerParams(vmem_limit_bytes=48 * 1024 * 1024),
        cost_estimate=pl.CostEstimate(flops=flops, bytes_accessed=moved, transcendentals=0),
    )(*operands)


def matmul(left, right):
    return jnp.dot(left, right, preferred_element_type=jnp.float32)


def taken_core(meta_ref, e, distance):
    return meta_ref[3] ^ (e >> 1) if distance == 2 else meta_ref[2] ^ (e & 1)


def level_of(meta_ref, slot, line):
    return lax.rem(meta_ref[0] + slot, line)


def place_rows(held_ref, lead, parts, levels, columns=slice(None)):
    half = held_ref.shape[-2] // 2
    done = 0
    for part in parts:
        for start in range(0, part.shape[0], half):
            slot, place = divmod(done + start, 2 * half)
            to = lead + (levels[slot], slice(place, place + half))
            held_ref[to] = part[start:start + half, columns]
        done += part.shape[0]


def left_products(mine_ref, right, out_ref, index):
    line, count, depth = mine_ref.shape
    size = line * count
    product = row_product(
        mine_ref[...].reshape(size, depth), right[...].reshape(size, depth)
    )
    out_ref[:, :, index * size:(index + 1) * size] = product.astype(out_ref.dtype).reshape(
        line, count, size
    )


def own_blocks_kernel(meta_ref, *refs):
    out_ref, mine_ref, pair_ref = refs[-3:]
    line = mine_ref.shape[0]
    levels = [level_of(meta_ref, i, line) for i in range(line)]
    place_rows(mine_ref, (), refs[:1], levels)
    place_rows(pair_ref, (), refs[1:2], levels)
    left_products(mine_ref, mine_ref, out_ref, 0)
    left_products(mine_ref, pair_ref, out_ref, 1)


def group_of(meta_ref, k, order):
    core = meta_ref[1] ^ k
    return (0, 1 + core, 2 - core, 3)[order]


def side_blocks_kernel(meta_ref, *refs):
    out_ref, mine_ref, right_ref = refs[-3:]
    line = mine_ref.shape[0]
    levels = [level_of(meta_ref, i, line) for i in range(line)]
    place_rows(mine_ref, (), refs[:1], levels)
    for d in (1, 2):
        for k in range(2):
            for order in (1, 2):
                is_core = taken_core(meta_ref, 0, d) == k

                @pl.when(jnp.logical_and(is_core, group_of(meta_ref, k, order) == d))
                def _():
                    place_rows(right_ref, (), [refs[2 * k + order]], levels)

        left_products(mine_ref, right_ref, out_ref, d - 1)


def corner_blocks_kernel(meta_ref, *refs):
    out_ref, mine_ref, right_ref = refs[-3:]
    line = mine_ref.shape[0]
    levels = [level_of(meta_ref, i, line) for i in range(line)]
    place_rows(mine_ref, (), refs[:1], levels)
    for k in range(2):

        @pl.when(taken_core(meta_ref, 0, 3) == k)
        def _():
            place_rows(right_ref, (), [refs[1 + k]], levels)

    left_products(mine_ref, right_ref, out_ref, 0)


def columns_kernel(slab, orders, meta_ref, *refs):
    out_ref, held_ref = refs[-2:]
    groups, _, line = held_ref.shape[:3]
    levels = [level_of(meta_ref, i, line) for i in range(line)]
    columns = pl.ds(pl.multiple_of(meta_ref[1] * slab, slab), slab)
    for k in range(2):
        for index, order in enumerate(orders):
            e = group_of(meta_ref, k, order) - orders[0]
            place_rows(held_ref, (e, k), [refs[len(orders) * k + index]], levels, columns)

    def step(i, carry):
        group, level = i // line, lax.rem(i, line)
        e, k = group // 2, lax.rem(group, 2)
        out_ref[e, k, level] = held_ref[e, k, level].T
        return carry

    lax.fori_loop(0, 2 * groups * line, step, 0)


def met_places(meta_ref, e, k):
    return [(e, k), (e, 1 - k)] + [(e ^ d, k ^ taken_core(meta_ref, e, d)) for d in (1, 2, 3)]


def side_by_side(turned_ref, places):
    line = turned_ref.shape[2]
    return jnp.concatenate(
        [turned_ref[a, b, level] for a, b in places for level in range(line)], axis=1
    )


def start_all(copies):
    for copy in copies:
        copy.start()
    return copies


def wait_all(copies):
    for copy in copies:
        copy.wait()


def shard_copies(meta_ref, refs, slots, held_ref, sems):
    copies = []
    for i, slot in enumerate(slots):
        for k in range(2):
            for order in range(4):
                source = refs[8 * slot + 4 * k + order]
                target = held_ref.at[group_of(meta_ref, k, order), k, i]
                copies.append(pltpu.make_async_copy(source, target, sems.at[len(copies)]))
    return copies


def column_copies(near_hbm, far_hbm, xt_ref, sems, used):
    parts = ((near_hbm, xt_ref.at[:3]), (far_hbm, xt_ref.at[3:]))
    return [
        pltpu.make_async_copy(source, target, sems.at[used + i])
        for i, (source, target) in enumerate(parts)
    ]


def by_columns(meta_ref, xt_ref, held_ref, levels, e, k):
    line, width, count = xt_ref.shape[2:]
    size = line * count
    left, right = [], []
    for d in (1, 2, 3):
        a = e ^ d
        b = k ^ taken_core(meta_ref, a, d)
        for n, level in enumerate(levels):
            left.append(xt_ref[a, b, level])
            right.append(held_ref[a, b, n, :, (1 + d) * size:(2 + d) * size])
    return matmul(jnp.concatenate(left, axis=1), jnp.concatenate(right))


def by_rows(meta_ref, xt_ref, held_ref, e, k):
    slots, count, width = held_ref.shape[2:]
    return row_product(
        side_by_side(xt_ref, met_places(meta_ref, e, k)),
        held_ref[e, k].reshape(slots * count, width),
    )


def when_held(copies, xt_copies, slots, body):
    wait_all(xt_copies)
    for e in range(4):
        if e == 1:
            wait_all([copies[8 * i + 4 * k + o] for i in range(slots) for k in (0, 1) for o in (1, 2)])
        if e in (0, 3):
            wait_all([copies[8 * i + 4 * k + e] for i in range(slots) for k in (0, 1)])

        def step(k, carry, e=e):
            body(e, k)
            return carry

        lax.fori_loop(0, 2, step, 0)


def image_parts(meta_ref, xt_ref, held_ref, levels, e, k):
    back = by_columns(meta_ref, xt_ref, held_ref, levels, e, k)
    return back, by_rows(meta_ref, xt_ref, held_ref, e, k)


def early_kernel(slots, meta_ref, near_hbm, far_hbm, *refs):
    acc_hbm, xt_ref, held_ref, acc_ref, sems, out_sems = refs[-6:]
    line, width, count = xt_ref.shape[2:]
    levels = [level_of(meta_ref, i, line) for i in range(slots)]
    copies = shard_copies(meta_ref, refs, range(slots), held_ref, sems)
    xt_copies = start_all(column_copies(near_hbm, far_hbm, xt_ref, sems, len(copies)))
    start_all(copies)
    other_levels = [level_of(meta_ref, i, line) for i in range(slots, line)]

    def rows_first(e, k):
        forth = by_rows(meta_ref, xt_ref, held_ref, e, k)
        for n, level in enumerate(levels):
            acc_ref[e, k, level] = forth[:, n * count:(n + 1) * count]
        for level in other_levels:
            acc_ref[e, k, level] = jnp.zeros((width, count), acc_ref.dtype)

    when_held(copies, xt_copies, slots, rows_first)

    def out_copy(i):
        return pltpu.make_async_copy(
            acc_ref.at[i // 2, lax.rem(i, 2)], acc_hbm.at[i // 2, lax.rem(i, 2)], out_sems.at[i]
        )

    def step(i, carry):
        e, k = i // 2, lax.rem(i, 2)
        back = by_columns(meta_ref, xt_ref, held_ref, levels, e, k)
        for level in range(line):
            acc_ref[e, k, level] += back[:, level * count:(level + 1) * count]
        out_copy(i).start()
        return carry

    lax.fori_loop(0, 8, step, 0)
    for i in range(8):
        out_copy(i).wait()


def last_kernel(gain, slots, meta_ref, near_hbm, far_hbm, acc_hbm, *refs):
    out_ref, xt_ref, held_ref, acc_ref, image_ref, own_ref, cross_ref, back_ref = refs[-11:-3]
    sems, acc_sems, later_sems = refs[-3:]
    line, width, count = xt_ref.shape[2:]
    size = line * count
    slot_levels = [level_of(meta_ref, i, line) for i in range(line)]
    levels = slot_levels[line - slots:]
    copies = shard_copies(meta_ref, refs, range(line - slots, line), held_ref, sems)
    copies += column_copies(near_hbm, far_hbm, xt_ref, sems, len(copies))
    start_all(copies)

    def acc_copy(i):
        held = lax.rem(i, 2)
        return pltpu.make_async_copy(
            acc_hbm.at[i // 2, held], acc_ref.at[held], acc_sems.at[held]
        )

    for i in range(2):
        acc_copy(i).start()
    later = []
    for i in range(line):
        for k in range(2):
            for order in range(4):
                source, target = refs[8 * i + 4 * k + order], own_ref.at[k, i]
                if order:
                    e = group_of(meta_ref, k, order)
                    first = (1 + e) * size
                    first = pl.multiple_of(first, size) if order < 3 else first
                    source, target = source.at[:, pl.ds(first, size)], cross_ref.at[e - 1, k, i]
                later.append(pltpu.make_async_copy(source, target, later_sems.at[len(later)]))
    start_all(later)
    wait_all(copies)

    def step(i, carry):
        e, k = i // 2, lax.rem(i, 2)
        back, forth = image_parts(meta_ref, xt_ref, held_ref, levels, e, k)
        acc_copy(i).wait()
        for n in range(slots):
            acc_ref[k, levels[n]] += forth[:, n * count:(n + 1) * count]
        for level in range(line):
            total = acc_ref[k, level] + back[:, level * count:(level + 1) * count]
            image_ref[e, k, level] = total.astype(jnp.bfloat16)

        @pl.when(i < 6)
        def _():
            acc_copy(i + 2).start()

        return carry

    lax.fori_loop(0, 8, step, 0)
    wait_all(later)

    def finish(k, carry):
        places = [(d, k ^ taken_core(meta_ref, d, d)) for d in (1, 2, 3)]
        blocks = [cross_ref[d - 1, b].reshape(size, size) for d, b in places]
        rows = [image_ref[d, b, level] for d, b in places for level in slot_levels]
        back = matmul(jnp.concatenate(rows, axis=1), jnp.concatenate(blocks))
        for level in range(line):
            back_ref[level] = back[:, level * count:(level + 1) * count]
        forth = row_product(
            side_by_side(image_ref, met_places(meta_ref, 0, k)),
            own_ref[k].reshape(size, 5 * size),
        )
        core = meta_ref[1] ^ k
        for i, level in enumerate(slot_levels):
            second = forth[:, i * count:(i + 1) * count] + back_ref[level]
            turned = combine(xt_ref[0, k, level], image_ref[0, k, level], second, gain)
            out_ref[level, core] = turned.T
        return carry

    lax.fori_loop(0, 2, finish, 0)


def after(values, *others):
    return lax.optimization_barrier((values,) + others)[0]


def neighbour_plan(iterate, gain):
    line = lax.axis_size("col") // 2
    count, width = iterate.shape
    slab = width // (2 * line)
    size = line * count
    row_devices = lax.axis_size("row")
    place, row = lax.axis_index("col"), lax.axis_index("row")
    level, core = place // 2, place % 2
    meta = jnp.stack([level, core, row & 1, row >> 1]).astype(jnp.int32)

    def along(values, hop):
        pairs = [(2 * a + k, 2 * ((a - hop) % line) + k) for a in range(line) for k in range(2)]
        return lax.ppermute(values, "col", pairs)

    def swap(values):
        pairs = [(2 * a + k, 2 * a + 1 - k) for a in range(line) for k in range(2)]
        return lax.ppermute(values, "col", pairs)

    def across(values, turn):
        pairs = [
            (r * 2 * line + c, (r ^ (1 + (c + turn) % 2)) * 2 * line + c)
            for r in range(row_devices)
            for c in range(2 * line)
        ]
        return lax.ppermute(values, ("row", "col"), pairs)

    def sent(partial):
        return [
            along(lax.dynamic_index_in_dim(partial, (level - hop) % line, 0, False), hop)
            for hop in range(1, line)
        ]

    def summed(partial, chunks):
        total = lax.dynamic_index_in_dim(partial, level, 0, False).astype(jnp.float32)
        for chunk in chunks:
            total += chunk.astype(jnp.float32)
        return total.astype(jnp.bfloat16)

    def piece(hop):
        start = ((level - hop) % line) * (2 * slab)
        return lax.dynamic_slice(iterate, (0, start), (count, 2 * slab))

    tower = jnp.concatenate(
        [along(piece(hop), hop) if hop else piece(0) for hop in range(line)]
    )
    pair_tower = swap(tower)
    flops = 4 * size * size * slab
    held = [pltpu.VMEM((line, count, 2 * slab), jnp.bfloat16)] * 2
    own_blocks = call(
        own_blocks_kernel,
        jax.ShapeDtypeStruct((line, count, 2 * size), jnp.bfloat16),
        [meta, tower, pair_tower],
        2 * flops,
        scratch=held,
    )
    own_shard = summed(own_blocks, sent(own_blocks))
    one, two = after(across(tower, 0), own_shard), after(across(tower, 1), own_shard)
    own_ring = along(own_shard, 1)
    own_one, own_two = across(own_shard, 0), across(own_shard, 1)
    pair_one, pair_two = swap(one), swap(two)
    side_blocks = call(
        side_blocks_kernel,
        jax.ShapeDtypeStruct((line, count, 2 * size), jnp.bfloat16),
        [meta, tower, one, two, pair_one, pair_two],
        2 * flops,
        scratch=held,
    )
    def columns(orders, *blocks):
        return call(
            functools.partial(columns_kernel, slab, orders),
            jax.ShapeDtypeStruct((len(orders), 2, line, slab, count), jnp.bfloat16),
            [after(meta, own_ring)] + list(blocks),
            size * slab * 128 * len(orders),
            scratch=[pltpu.VMEM((len(orders), 2, line, count, slab), jnp.bfloat16)],
        )

    side_sent = sent(side_blocks)
    near_columns = columns((0, 1, 2), tower, one, two, pair_tower, pair_one, pair_two)
    three = after(across(one, 1), side_sent[0], side_sent[-1], near_columns)
    pair_three = swap(three)
    corner_blocks = call(
        corner_blocks_kernel,
        jax.ShapeDtypeStruct((line, count, size), jnp.bfloat16),
        [meta, tower, three, pair_three],
        flops,
        scratch=held,
    )
    far_columns = columns((3,), three, pair_three)
    side_shard = summed(side_blocks, side_sent)
    own_three = across(own_one, 1)
    corner_sent = [after(chunk, own_two, own_three, far_columns) for chunk in sent(corner_blocks)]
    corner_shard = summed(corner_blocks, corner_sent)
    cross_shard = jnp.concatenate([side_shard, corner_shard], axis=1)

    cut = line // 2
    turned = (4, 2, line, slab, count)

    def wide(own, cross):
        return jnp.concatenate([own, cross], axis=1)

    cross_ring = along(cross_shard, 1)
    cross_one, cross_two = across(cross_shard, 0), across(cross_shard, 1)
    held_back = [cross_ring, cross_one, cross_two]
    near = [wide(own_shard, cross_shard), wide(own_ring, after(cross_ring, *held_back))]
    one, two = [wide(own_one, cross_one)], [wide(own_two, cross_two)]
    three, ring = [], [near[1]]

    def pieces(slots):
        own = [[near[i], one[i], two[i], three[i]] for i in slots]
        return [v for blocks in own for v in blocks + [swap(block) for block in blocks]]

    def early():
        return call(
            functools.partial(early_kernel, cut),
            jax.ShapeDtypeStruct(turned, jnp.float32),
            [meta, near_columns, far_columns] + pieces(range(cut)),
            128 * cut * count * size * slab,
            scratch=[
                pltpu.VMEM(turned, jnp.bfloat16),
                pltpu.VMEM((4, 2, cut, count, 5 * size), jnp.bfloat16),
                pltpu.VMEM(turned, jnp.float32),
                pltpu.SemaphoreType.DMA((8 * cut + 2,)),
                pltpu.SemaphoreType.DMA((8,)),
            ],
            space=pltpu.HBM,
            out_space=pltpu.HBM,
        )

    late = line - 2 if line > 3 else line
    for step in range(1, line + 1):
        done = held_back if step == 1 else [b[-1] for b in (ring, one, two, three)]
        if step == line:
            acc = early()
            done = done + [two[-2], acc]
        if step == 1:
            cross_three = across(after(cross_one, *done), 1)
            three.append(wide(own_three, cross_three))
        elif step == late + 1:
            two.append(across(after(near[late], *done), 1))
            three.append(along(after(three[-1], *done), 1))
        else:
            three.append(across(after(one[-1], *done), 1))
        if step < line:
            here = after(near[step], *done)
            one.append(across(here, 0))
            if step != late:
                two.append(across(here, 1))
        if step < line - 1:
            ring.append(along(here, 1))
            near.append(ring[-1])
    update = call(
        functools.partial(last_kernel, gain, line - cut),
        jax.ShapeDtypeStruct((line, 2, count, slab), jnp.bfloat16),
        [meta, near_columns, far_columns, acc] + pieces(range(line)),
        (128 * (line - cut) * count + 32 * size) * size * slab,
        scratch=[
            pltpu.VMEM(turned, jnp.bfloat16),
            pltpu.VMEM((4, 2, line - cut, count, 5 * size), jnp.bfloat16),
            pltpu.VMEM((2, line, slab, count), jnp.float32),
            pltpu.VMEM(turned, jnp.bfloat16),
            pltpu.VMEM((2, line, count, 5 * size), jnp.bfloat16),
            pltpu.VMEM((3, 2, line, count, size), jnp.bfloat16),
            pltpu.VMEM((line, slab, count), jnp.float32),
            pltpu.SemaphoreType.DMA((8 * (line - cut) + 2,)),
            pltpu.SemaphoreType.DMA((2,)),
            pltpu.SemaphoreType.DMA((8 * line,)),
        ],
        space=pltpu.HBM,
    )
    return update.reshape(2 * size, slab)


def solution(mesh):
    square_of_lines = mesh.shape["row"] == 4 and mesh.shape["col"] in (4, 6, 8)

    def program(iterate):
        gain = output_gain * math.sqrt(max(iterate.shape))
        plan = neighbour_plan if square_of_lines else gathered_plan
        return jax.shard_map(
            lambda block: plan(block, gain),
            mesh=mesh,
            in_specs=(P(("row", "col"), None),),
            out_specs=P("row", "col"),
            check_vma=False,
        )(iterate)

    return program
```

```python
import functools
import math

import jax
import jax.numpy as jnp
from jax import lax
from jax.experimental import pallas as pl
from jax.experimental.pallas import tpu as pltpu
from jax.sharding import PartitionSpec as P

linear_weight = 3.4445
cubic_weight = -4.775
quintic_weight = 2.0315
output_gain = 0.2


def gather_rows(block_rows):
    return lax.all_gather(block_rows, "row", axis=0, tiled=True)


def strided_order(panel_rows, row_devices, col_devices):
    total_rows, column_count = panel_rows.shape
    per_device = total_rows // (row_devices * col_devices)
    grouped = panel_rows.reshape(row_devices, col_devices, per_device, column_count)
    return jnp.transpose(grouped, (1, 0, 2, 3)).reshape(total_rows, column_count)


def row_product(left_rows, right_rows):
    return lax.dot_general(
        left_rows, right_rows, (((1,), (1,)), ((), ())), preferred_element_type=jnp.float32
    )


def combine(scaled_tile, image_tile, second_term, gain):
    combined = (
        linear_weight * scaled_tile.astype(jnp.float32)
        + cubic_weight * image_tile.astype(jnp.float32)
        + quintic_weight * second_term
    )
    return (gain * combined).astype(jnp.bfloat16)


def gathered_plan(iterate, gain):
    scaled_tile = lax.all_to_all(iterate, "col", split_axis=1, concat_axis=0, tiled=True)
    row_devices = lax.axis_size("row")
    col_devices = lax.axis_size("col")
    strided_rows = gather_rows(iterate)
    panel_rows = lax.all_gather(scaled_tile, "col", axis=1, tiled=True)
    gram_tile = row_product(panel_rows, strided_rows).astype(jnp.bfloat16)
    gram_wide = lax.all_gather(gram_tile, "col", axis=1, tiled=True)
    scaled_columns = strided_order(gather_rows(scaled_tile), row_devices, col_devices)
    image_tile = jnp.dot(gram_wide, scaled_columns, preferred_element_type=jnp.float32).astype(
        jnp.bfloat16
    )
    image_columns = strided_order(gather_rows(image_tile), row_devices, col_devices)
    second_term = jnp.dot(gram_wide, image_columns, preferred_element_type=jnp.float32)
    return combine(scaled_tile, image_tile, second_term, gain)


def call(
    kernel, out_shape, operands, flops, scratch=(), space=pltpu.VMEM, out_space=pltpu.VMEM
):
    specs = [pl.BlockSpec(memory_space=pltpu.SMEM)]
    specs += [pl.BlockSpec(memory_space=space)] * (len(operands) - 1)
    moved = sum(math.prod(v.shape) * v.dtype.itemsize for v in operands)
    return pl.pallas_call(
        kernel,
        in_specs=specs,
        out_specs=pl.BlockSpec(memory_space=out_space),
        out_shape=out_shape,
        scratch_shapes=list(scratch),
        compiler_params=pltpu.CompilerParams(vmem_limit_bytes=48 * 1024 * 1024),
        cost_estimate=pl.CostEstimate(flops=flops, bytes_accessed=moved, transcendentals=0),
    )(*operands)


def matmul(left, right):
    return jnp.dot(left, right, preferred_element_type=jnp.float32)


def taken_core(meta_ref, e, distance):
    return meta_ref[3] ^ (e >> 1) if distance == 2 else meta_ref[2] ^ (e & 1)


def level_of(meta_ref, slot, line):
    return lax.rem(meta_ref[0] + slot, line)


def place_rows(held_ref, lead, parts, levels, columns=slice(None)):
    half = held_ref.shape[-2] // 2
    done = 0
    for part in parts:
        for start in range(0, part.shape[0], half):
            slot, place = divmod(done + start, 2 * half)
            to = lead + (levels[slot], slice(place, place + half))
            held_ref[to] = part[start:start + half, columns]
        done += part.shape[0]


def left_products(mine_ref, right, out_ref, index):
    line, count, depth = mine_ref.shape
    size = line * count
    product = row_product(
        mine_ref[...].reshape(size, depth), right[...].reshape(size, depth)
    )
    out_ref[:, :, index * size:(index + 1) * size] = product.astype(out_ref.dtype).reshape(
        line, count, size
    )


def own_blocks_kernel(meta_ref, *refs):
    out_ref, mine_ref, pair_ref = refs[-3:]
    line = mine_ref.shape[0]
    levels = [level_of(meta_ref, i, line) for i in range(line)]
    place_rows(mine_ref, (), refs[:1], levels)
    place_rows(pair_ref, (), refs[1:2], levels)
    left_products(mine_ref, mine_ref, out_ref, 0)
    left_products(mine_ref, pair_ref, out_ref, 1)


def group_of(meta_ref, k, order):
    core = meta_ref[1] ^ k
    return (0, 1 + core, 2 - core, 3)[order]


def side_blocks_kernel(meta_ref, *refs):
    out_ref, mine_ref, right_ref = refs[-3:]
    line = mine_ref.shape[0]
    levels = [level_of(meta_ref, i, line) for i in range(line)]
    place_rows(mine_ref, (), refs[:1], levels)
    for d in (1, 2):
        for k in range(2):
            for order in (1, 2):
                is_core = taken_core(meta_ref, 0, d) == k

                @pl.when(jnp.logical_and(is_core, group_of(meta_ref, k, order) == d))
                def _():
                    place_rows(right_ref, (), [refs[2 * k + order]], levels)

        left_products(mine_ref, right_ref, out_ref, d - 1)


def corner_blocks_kernel(meta_ref, *refs):
    out_ref, mine_ref, right_ref = refs[-3:]
    line = mine_ref.shape[0]
    levels = [level_of(meta_ref, i, line) for i in range(line)]
    place_rows(mine_ref, (), refs[:1], levels)
    for k in range(2):

        @pl.when(taken_core(meta_ref, 0, 3) == k)
        def _():
            place_rows(right_ref, (), [refs[1 + k]], levels)

    left_products(mine_ref, right_ref, out_ref, 0)


def columns_kernel(slab, orders, meta_ref, *refs):
    out_ref, held_ref = refs[-2:]
    groups, _, line = held_ref.shape[:3]
    levels = [level_of(meta_ref, i, line) for i in range(line)]
    columns = pl.ds(pl.multiple_of(meta_ref[1] * slab, slab), slab)
    for k in range(2):
        for index, order in enumerate(orders):
            e = group_of(meta_ref, k, order) - orders[0]
            place_rows(held_ref, (e, k), [refs[len(orders) * k + index]], levels, columns)

    def step(i, carry):
        group, level = i // line, lax.rem(i, line)
        e, k = group // 2, lax.rem(group, 2)
        out_ref[e, k, level] = held_ref[e, k, level].T
        return carry

    lax.fori_loop(0, 2 * groups * line, step, 0)


def met_places(meta_ref, e, k):
    return [(e, k), (e, 1 - k)] + [(e ^ d, k ^ taken_core(meta_ref, e, d)) for d in (1, 2, 3)]


def side_by_side(turned_ref, places):
    line = turned_ref.shape[2]
    return jnp.concatenate(
        [turned_ref[a, b, level] for a, b in places for level in range(line)], axis=1
    )


def start_all(copies):
    for copy in copies:
        copy.start()
    return copies


def wait_all(copies):
    for copy in copies:
        copy.wait()


def shard_copies(meta_ref, refs, slots, held_ref, sems):
    copies = []
    for i, slot in enumerate(slots):
        for k in range(2):
            for order in range(4):
                source = refs[8 * slot + 4 * k + order]
                target = held_ref.at[group_of(meta_ref, k, order), k, i]
                copies.append(pltpu.make_async_copy(source, target, sems.at[len(copies)]))
    return copies


def column_copies(near_hbm, far_hbm, xt_ref, sems, used):
    parts = ((near_hbm, xt_ref.at[:3]), (far_hbm, xt_ref.at[3:]))
    return [
        pltpu.make_async_copy(source, target, sems.at[used + i])
        for i, (source, target) in enumerate(parts)
    ]


def by_columns(meta_ref, xt_ref, held_ref, levels, e, k):
    line, width, count = xt_ref.shape[2:]
    size = line * count
    left, right = [], []
    for d in (1, 2, 3):
        a = e ^ d
        b = k ^ taken_core(meta_ref, a, d)
        for n, level in enumerate(levels):
            left.append(xt_ref[a, b, level])
            right.append(held_ref[a, b, n, :, (1 + d) * size:(2 + d) * size])
    return matmul(jnp.concatenate(left, axis=1), jnp.concatenate(right))


def by_rows(meta_ref, xt_ref, held_ref, e, k):
    slots, count, width = held_ref.shape[2:]
    return row_product(
        side_by_side(xt_ref, met_places(meta_ref, e, k)),
        held_ref[e, k].reshape(slots * count, width),
    )


def when_held(copies, xt_copies, slots, body):
    wait_all(xt_copies)
    for e in range(4):
        if e == 1:
            wait_all([copies[8 * i + 4 * k + o] for i in range(slots) for k in (0, 1) for o in (1, 2)])
        if e in (0, 3):
            wait_all([copies[8 * i + 4 * k + e] for i in range(slots) for k in (0, 1)])

        def step(k, carry, e=e):
            body(e, k)
            return carry

        lax.fori_loop(0, 2, step, 0)


def image_parts(meta_ref, xt_ref, held_ref, levels, e, k):
    back = by_columns(meta_ref, xt_ref, held_ref, levels, e, k)
    return back, by_rows(meta_ref, xt_ref, held_ref, e, k)


def early_kernel(slots, meta_ref, near_hbm, far_hbm, *refs):
    acc_hbm, xt_ref, held_ref, acc_ref, sems, out_sems = refs[-6:]
    line, width, count = xt_ref.shape[2:]
    levels = [level_of(meta_ref, i, line) for i in range(slots)]
    copies = shard_copies(meta_ref, refs, range(slots), held_ref, sems)
    xt_copies = start_all(column_copies(near_hbm, far_hbm, xt_ref, sems, len(copies)))
    start_all(copies)
    other_levels = [level_of(meta_ref, i, line) for i in range(slots, line)]

    def rows_first(e, k):
        forth = by_rows(meta_ref, xt_ref, held_ref, e, k)
        for n, level in enumerate(levels):
            acc_ref[e, k, level] = forth[:, n * count:(n + 1) * count]
        for level in other_levels:
            acc_ref[e, k, level] = jnp.zeros((width, count), acc_ref.dtype)

    when_held(copies, xt_copies, slots, rows_first)

    def out_copy(i):
        return pltpu.make_async_copy(
            acc_ref.at[i // 2, lax.rem(i, 2)], acc_hbm.at[i // 2, lax.rem(i, 2)], out_sems.at[i]
        )

    def step(i, carry):
        e, k = i // 2, lax.rem(i, 2)
        back = by_columns(meta_ref, xt_ref, held_ref, levels, e, k)
        for level in range(line):
            acc_ref[e, k, level] += back[:, level * count:(level + 1) * count]
        out_copy(i).start()
        return carry

    lax.fori_loop(0, 8, step, 0)
    for i in range(8):
        out_copy(i).wait()


def last_kernel(gain, slots, meta_ref, near_hbm, far_hbm, acc_hbm, *refs):
    out_ref, xt_ref, held_ref, acc_ref, image_ref, own_ref, cross_ref, back_ref = refs[-11:-3]
    sems, acc_sems, later_sems = refs[-3:]
    line, width, count = xt_ref.shape[2:]
    size = line * count
    slot_levels = [level_of(meta_ref, i, line) for i in range(line)]
    levels = slot_levels[line - slots:]
    copies = shard_copies(meta_ref, refs, range(line - slots, line), held_ref, sems)
    copies += column_copies(near_hbm, far_hbm, xt_ref, sems, len(copies))
    start_all(copies)

    def acc_copy(i):
        held = lax.rem(i, 2)
        return pltpu.make_async_copy(
            acc_hbm.at[i // 2, held], acc_ref.at[held], acc_sems.at[held]
        )

    later = []
    for i in range(line):
        for k in range(2):
            for order in range(4):
                source, target = refs[8 * i + 4 * k + order], own_ref.at[k, i]
                if order:
                    e = group_of(meta_ref, k, order)
                    first = (1 + e) * size
                    first = pl.multiple_of(first, size) if order < 3 else first
                    source, target = source.at[:, pl.ds(first, size)], cross_ref.at[e - 1, k, i]
                later.append(pltpu.make_async_copy(source, target, later_sems.at[len(later)]))
    wait_all(copies)
    for i in range(2):
        acc_copy(i).start()
    start_all(later)

    def step(i, carry):
        e, k = i // 2, lax.rem(i, 2)
        back, forth = image_parts(meta_ref, xt_ref, held_ref, levels, e, k)
        acc_copy(i).wait()
        for n in range(slots):
            acc_ref[k, levels[n]] += forth[:, n * count:(n + 1) * count]
        for level in range(line):
            total = acc_ref[k, level] + back[:, level * count:(level + 1) * count]
            image_ref[e, k, level] = total.astype(jnp.bfloat16)

        @pl.when(i < 6)
        def _():
            acc_copy(i + 2).start()

        return carry

    lax.fori_loop(0, 8, step, 0)
    wait_all(later)

    def finish(k, carry):
        places = [(d, k ^ taken_core(meta_ref, d, d)) for d in (1, 2, 3)]
        blocks = [cross_ref[d - 1, b].reshape(size, size) for d, b in places]
        rows = [image_ref[d, b, level] for d, b in places for level in slot_levels]
        back = matmul(jnp.concatenate(rows, axis=1), jnp.concatenate(blocks))
        for level in range(line):
            back_ref[level] = back[:, level * count:(level + 1) * count]
        forth = row_product(
            side_by_side(image_ref, met_places(meta_ref, 0, k)),
            own_ref[k].reshape(size, 5 * size),
        )
        core = meta_ref[1] ^ k
        for i, level in enumerate(slot_levels):
            second = forth[:, i * count:(i + 1) * count] + back_ref[level]
            turned = combine(xt_ref[0, k, level], image_ref[0, k, level], second, gain)
            out_ref[level, core] = turned.T
        return carry

    lax.fori_loop(0, 2, finish, 0)


def after(values, *others):
    return lax.optimization_barrier((values,) + others)[0]


def neighbour_plan(iterate, gain):
    line = lax.axis_size("col") // 2
    count, width = iterate.shape
    slab = width // (2 * line)
    size = line * count
    row_devices = lax.axis_size("row")
    place, row = lax.axis_index("col"), lax.axis_index("row")
    level, core = place // 2, place % 2
    meta = jnp.stack([level, core, row & 1, row >> 1]).astype(jnp.int32)

    def along(values, hop):
        pairs = [(2 * a + k, 2 * ((a - hop) % line) + k) for a in range(line) for k in range(2)]
        return lax.ppermute(values, "col", pairs)

    def swap(values):
        pairs = [(2 * a + k, 2 * a + 1 - k) for a in range(line) for k in range(2)]
        return lax.ppermute(values, "col", pairs)

    def across(values, turn):
        pairs = [
            (r * 2 * line + c, (r ^ (1 + (c + turn) % 2)) * 2 * line + c)
            for r in range(row_devices)
            for c in range(2 * line)
        ]
        return lax.ppermute(values, ("row", "col"), pairs)

    def sent(partial):
        return [
            along(lax.dynamic_index_in_dim(partial, (level - hop) % line, 0, False), hop)
            for hop in range(1, line)
        ]

    def summed(partial, chunks):
        total = lax.dynamic_index_in_dim(partial, level, 0, False).astype(jnp.float32)
        for chunk in chunks:
            total += chunk.astype(jnp.float32)
        return total.astype(jnp.bfloat16)

    def piece(hop):
        start = ((level - hop) % line) * (2 * slab)
        return lax.dynamic_slice(iterate, (0, start), (count, 2 * slab))

    tower = jnp.concatenate(
        [along(piece(hop), hop) if hop else piece(0) for hop in range(line)]
    )
    pair_tower = swap(tower)
    flops = 4 * size * size * slab
    held = [pltpu.VMEM((line, count, 2 * slab), jnp.bfloat16)] * 2
    own_blocks = call(
        own_blocks_kernel,
        jax.ShapeDtypeStruct((line, count, 2 * size), jnp.bfloat16),
        [meta, tower, pair_tower],
        2 * flops,
        scratch=held,
    )
    own_shard = summed(own_blocks, sent(own_blocks))
    one, two = after(across(tower, 0), own_shard), after(across(tower, 1), own_shard)
    own_ring = along(own_shard, 1)
    own_one, own_two = across(own_shard, 0), across(own_shard, 1)
    pair_one, pair_two = swap(one), swap(two)
    side_blocks = call(
        side_blocks_kernel,
        jax.ShapeDtypeStruct((line, count, 2 * size), jnp.bfloat16),
        [meta, tower, one, two, pair_one, pair_two],
        2 * flops,
        scratch=held,
    )
    def columns(orders, *blocks):
        return call(
            functools.partial(columns_kernel, slab, orders),
            jax.ShapeDtypeStruct((len(orders), 2, line, slab, count), jnp.bfloat16),
            [after(meta, own_ring)] + list(blocks),
            size * slab * 128 * len(orders),
            scratch=[pltpu.VMEM((len(orders), 2, line, count, slab), jnp.bfloat16)],
        )

    side_sent = sent(side_blocks)
    near_columns = columns((0, 1, 2), tower, one, two, pair_tower, pair_one, pair_two)
    three = after(across(one, 1), side_sent[0], side_sent[-1], near_columns)
    pair_three = swap(three)
    corner_blocks = call(
        corner_blocks_kernel,
        jax.ShapeDtypeStruct((line, count, size), jnp.bfloat16),
        [meta, tower, three, pair_three],
        flops,
        scratch=held,
    )
    far_columns = columns((3,), three, pair_three)
    side_shard = summed(side_blocks, side_sent)
    own_three = across(own_one, 1)
    corner_sent = [after(chunk, own_two, own_three, far_columns) for chunk in sent(corner_blocks)]
    corner_shard = summed(corner_blocks, corner_sent)
    cross_shard = jnp.concatenate([side_shard, corner_shard], axis=1)

    cut = line // 2
    turned = (4, 2, line, slab, count)

    def wide(own, cross):
        return jnp.concatenate([own, cross], axis=1)

    cross_ring = along(cross_shard, 1)
    cross_one, cross_two = across(cross_shard, 0), across(cross_shard, 1)
    held_back = [cross_ring, cross_one, cross_two]
    near = [wide(own_shard, cross_shard), wide(own_ring, after(cross_ring, *held_back))]
    one, two = [wide(own_one, cross_one)], [wide(own_two, cross_two)]
    three, ring = [], [near[1]]

    def pieces(slots):
        own = [[near[i], one[i], two[i], three[i]] for i in slots]
        return [v for blocks in own for v in blocks + [swap(block) for block in blocks]]

    def early():
        return call(
            functools.partial(early_kernel, cut),
            jax.ShapeDtypeStruct(turned, jnp.float32),
            [meta, near_columns, far_columns] + pieces(range(cut)),
            128 * cut * count * size * slab,
            scratch=[
                pltpu.VMEM(turned, jnp.bfloat16),
                pltpu.VMEM((4, 2, cut, count, 5 * size), jnp.bfloat16),
                pltpu.VMEM(turned, jnp.float32),
                pltpu.SemaphoreType.DMA((8 * cut + 2,)),
                pltpu.SemaphoreType.DMA((8,)),
            ],
            space=pl.ANY,
            out_space=pl.ANY,
        )

    late = line - 2 if line > 3 else line
    for step in range(1, line + 1):
        done = held_back if step == 1 else [b[-1] for b in (ring, one, two, three)]
        if step == line:
            acc = early()
            done = done + [two[-2], acc]
        if step == 1:
            cross_three = across(after(cross_one, *done), 1)
            three.append(wide(own_three, cross_three))
        elif step == late + 1:
            two.append(across(after(near[late], *done), 1))
            three.append(along(after(three[-1], *done), 1))
        else:
            three.append(across(after(one[-1], *done), 1))
        if step < line:
            here = after(near[step], *done)
            one.append(across(here, 0))
            if step != late:
                two.append(across(here, 1))
        if step < line - 1:
            ring.append(along(here, 1))
            near.append(ring[-1])
    update = call(
        functools.partial(last_kernel, gain, line - cut),
        jax.ShapeDtypeStruct((line, 2, count, slab), jnp.bfloat16),
        [meta, near_columns, far_columns, acc] + pieces(range(line)),
        (128 * (line - cut) * count + 32 * size) * size * slab,
        scratch=[
            pltpu.VMEM(turned, jnp.bfloat16),
            pltpu.VMEM((4, 2, line - cut, count, 5 * size), jnp.bfloat16),
            pltpu.VMEM((2, line, slab, count), jnp.float32),
            pltpu.VMEM(turned, jnp.bfloat16),
            pltpu.VMEM((2, line, count, 5 * size), jnp.bfloat16),
            pltpu.VMEM((3, 2, line, count, size), jnp.bfloat16),
            pltpu.VMEM((line, slab, count), jnp.float32),
            pltpu.SemaphoreType.DMA((8 * (line - cut) + 2,)),
            pltpu.SemaphoreType.DMA((2,)),
            pltpu.SemaphoreType.DMA((8 * line,)),
        ],
        space=pl.ANY,
    )
    return update.reshape(2 * size, slab)


def solution(mesh):
    square_of_lines = mesh.shape["row"] == 4 and mesh.shape["col"] in (4, 6, 8)

    def program(iterate):
        gain = output_gain * math.sqrt(max(iterate.shape))
        plan = neighbour_plan if square_of_lines else gathered_plan
        return jax.shard_map(
            lambda block: plan(block, gain),
            mesh=mesh,
            in_specs=(P(("row", "col"), None),),
            out_specs=P("row", "col"),
            check_vma=False,
        )(iterate)

    return program
```
